32 devices in a mesh: seq: 8 (over z, y), ex: 4 (over x, core).
Axes of the slice: x: 2, y: 2, z: 4, core: 2. Of those that a mesh axis runs over, the one named last changes fastest.
Arguments:
- block_input: float32 [16, 1024, 768], P('ex', 'seq'), may hold values from -6 to 6
- segment_ids: int32 [16, 1024], P('ex'), may hold values from 0 to 1, as said below
- expert_ids: int32 [16, 1024, 1], P('ex', 'seq'), may hold values from 0 to 3; in each aligned block of 128 rows (0 to 127, 128 to 255, ..., all dimensions but the last counted through in order) at most 48 rows name the same one
- ln1_gain: float32 [768], replicated, may hold values from 0.5 to 1.5
- ln1_bias: float32 [768], replicated, may hold values from -1 to 1
- ln2_gain: float32 [768], replicated, may hold values from 0.5 to 1.5
- ln2_bias: float32 [768], replicated, may hold values from -1 to 1
- w_qkv: bfloat16 [768, 2304], replicated, may hold values from -0.3125 to 0.3125
- w_attn_out: bfloat16 [768, 768], replicated, may hold values from -1.75 to 1.75
- w_in: bfloat16 [4, 768, 3072], P('ex'), may hold values from -0.21875 to 0.21875
- w_down: bfloat16 [4, 3072, 768], P('ex'), may hold values from -0.15625 to 0.15625
- grad_out: float32 [16, 1024, 768], P('ex', 'seq'), may hold values from -6 to 6
Outputs:
- block_output: float32 [16, 1024, 768], P('ex', 'seq')
- grad_input: float32 [16, 1024, 768], P('ex', 'seq')
- grad_w_qkv: float32 [768, 2304], replicated
- grad_w_attn_out: float32 [768, 768], replicated
- grad_ln1_gain: float32 [768], replicated
- grad_ln1_bias: float32 [768], replicated
- grad_ln2_gain: float32 [768], replicated
- grad_ln2_bias: float32 [768], replicated
- grad_w_in: float32 [4, 768, 3072], P('ex')
- grad_w_down: float32 [4, 3072, 768], P('ex')
- expert_load: float32 [4], replicated
The draws below stay inside these ranges and needn't reach their ends.
Inputs may be any that keep to these rules, and one draw needn't show every extreme that they name: `segment_ids`: Non-decreasing along each row and starting at 0; in each aligned group of 4 rows one row is a single document. `expert_ids`: in each aligned block of 128 positions of a row (the positions of one device in that row) at most 48 tokens name one expert.
All inputs are finite; a program needn't handle non-finite values.
Results may differ from the reference program's by a relative error of at most 0.04.
Values may be sent and summed in bfloat16 or wider, within the bound.
No kernel may reach another device: no remote copies, remote signals or barrier semaphores. Data moves between devices by JAX's collectives and lax.ppermute only.
A program may use at most 320 MiB of HBM per device.

```python
import math
import jax
import jax.numpy as jnp
import numpy as np
from jax import lax

D = 768
HEADS = 12
HEAD = 64
FF = 3072
SEQ_DEV = 128
ROW_DEV = 4
DOC = 1024
EXPERTS = 4
MOST = 48
ROWS = 16
LENGTH = 1024


def draw_segment_ids(key, part):
    key = jax.random.fold_in(key, 7)
    first_key, second_key = jax.random.split(key)
    count = max(LENGTH // DOC, 2)
    spacing = LENGTH // count
    position = jnp.arange(LENGTH, dtype=jnp.int32)
    jitter = jax.random.randint(first_key, (ROWS, count), -(spacing // 4), spacing // 4 + 1)
    bounds = jnp.arange(1, count + 1, dtype=jnp.int32)[None, :] * spacing + jitter
    labels = jnp.sum((position[None, :, None] >= bounds[:, None, :]).astype(jnp.int32), -1)
    labels = jnp.minimum(labels, count - 1)
    picked = jax.random.randint(second_key, (ROWS // ROW_DEV,), 0, ROW_DEV)
    single = jnp.arange(ROWS, dtype=jnp.int32) % ROW_DEV == jnp.repeat(picked, ROW_DEV)
    return jnp.where(single[:, None], 0, labels)


def steps_of(rng, shape, cuts, least, largest):
    level, own = 1.0, jax.random.fold_in(rng, 6)
    for dim, blocks in cuts:
        draws = jnp.exp(jax.random.uniform(jax.random.fold_in(own, dim), (blocks,), jnp.float32, least / len(cuts), largest / len(cuts)))
        level = level * jnp.repeat(draws, shape[dim] // blocks).reshape([-1 if axis == dim else 1 for axis in range(len(shape))])
    return level


def shared_out(rng, own, number, rows, count, top, reach, lean):
    ranking = jax.random.permutation(rng, count)
    heavy_load, common = portions_of(count, rows * top, reach, lean, True), portions_of(count, rows * top, reach, lean, False)
    places = jnp.arange(count)

    def named(sizes, turn):
        used = int((sizes > 0).sum())
        fixed = max(1, used // 4)
        passed = fixed + (places - fixed + turn * (used - fixed)) % max(1, count - fixed)
        return jnp.zeros((count,), jnp.int32).at[ranking[jnp.where(places < fixed, places, passed)]].set(jnp.asarray(sizes, jnp.int32))

    sizes = jnp.where(number % 4 == 0, named(heavy_load, number // 4), named(common, number - number // 4 - 1))
    mixed = jax.random.permutation(jax.random.fold_in(own, 3), count)
    giver, sink = mixed[0:count // 2 * 2:2], mixed[1:count // 2 * 2:2]
    room = jnp.minimum(sizes[giver] - 1, reach - sizes[sink]) // 2
    room = jnp.where((giver == ranking[0]) | (sink == ranking[0]) | (sizes[sink] == 0), 0, jnp.maximum(room, 0))
    passed = jax.random.randint(jax.random.fold_in(own, 4), (count // 2,), 0, 1 << 20) % (room + 1)
    sizes = sizes.at[giver].add(-passed).at[sink].add(passed)
    items = jnp.searchsorted(jnp.cumsum(sizes), jnp.arange(rows * top), side="right").astype(jnp.int32)
    table = items.reshape(top, rows).T
    table = table[jax.random.permutation(jax.random.fold_in(own, 1), rows)]
    turn = jax.random.randint(jax.random.fold_in(own, 2), (rows, 1), 0, top)
    return jnp.take_along_axis(table, (jnp.arange(top)[None, :] + turn) % top, axis=1)


def portions_of(count, total, limit, skew, full):
    loads = [(1 << 20) // math.isqrt(grade ** skew) + 1 for grade in range(1, count + 1)]
    largest = limit if full else min(limit, max(-(-total // count), total * loads[0] // sum(loads)))
    least = 1 if total - largest >= count - 1 else 0
    holding, surplus = [largest] + [least] * (count - 1), total - largest - least * (count - 1)
    while surplus > 0:
        movable = [i for i in range(1, count) if holding[i] < largest] or [i for i in range(1, count) if holding[i] < limit]
        pool, remaining = sum([loads[i] for i in movable]), surplus
        for i in movable:
            more = min(limit - holding[i], max(1, remaining * loads[i] // pool), surplus)
            holding[i] = holding[i] + more
            surplus = surplus - more
    return np.array(holding)


def noise(own_key, extent, width, limit, cuts=(), kind=jnp.bfloat16):
    array = jax.random.normal(own_key, extent, jnp.float32) * width
    if len(cuts) > 0:
        array = steps_of(own_key, extent, cuts, -0.22, 0.18) * array
    return jnp.clip(array, min=-limit, max=limit).astype(kind)


def setup_inputs(seed: int = 0) -> dict:
    splits = jax.random.split(jax.random.key(seed), 13)
    block_input = noise(splits[0], (ROWS, LENGTH, D), 1.0, 6.0, ((0, 4), (1, 8)), jnp.float32)
    segment_ids = draw_segment_ids(jax.random.fold_in(splits[12], 71), 0)
    expert_ids_keys = jax.random.split(jax.random.fold_in(splits[2], 1), ROWS * LENGTH // SEQ_DEV)
    expert_ids_turns = jax.random.permutation(jax.random.fold_in(splits[2], 3), ROWS * LENGTH // SEQ_DEV)
    expert_ids = jax.vmap(lambda own, number: shared_out(jax.random.fold_in(splits[2], 2), own, number, SEQ_DEV, EXPERTS, 1, MOST, 1))(expert_ids_keys, expert_ids_turns).reshape((ROWS, LENGTH, 1))
    ln1_gain = jnp.clip(1.0 + 0.1 * jax.random.normal(splits[3], (D,), jnp.float32), 0.5, 1.5)
    ln1_bias = noise(splits[4], (D,), 0.2, 1.0, (), jnp.float32)
    ln2_gain = jnp.clip(1.0 + 0.1 * jax.random.normal(splits[5], (D,), jnp.float32), 0.5, 1.5)
    ln2_bias = noise(splits[6], (D,), 0.2, 1.0, (), jnp.float32)
    w_qkv = noise(splits[7], (D, 3 * D), (D // 2) ** -0.5, 0.3125)
    w_attn_out = noise(splits[8], (D, D), (D // 64) ** -0.5, 1.75)
    w_in = noise(splits[9], (EXPERTS, D, FF), D ** -0.5, 0.21875, ((0, 4),))
    w_down = noise(splits[10], (EXPERTS, FF, D), (FF // 2) ** -0.5, 0.15625, ((0, 4),))
    grad_out = noise(splits[11], (ROWS, LENGTH, D), 1.0, 6.0, ((0, 4), (1, 8)), jnp.float32)
    return {"block_input": block_input, "segment_ids": segment_ids, "expert_ids": expert_ids, "ln1_gain": ln1_gain, "ln1_bias": ln1_bias, "ln2_gain": ln2_gain, "ln2_bias": ln2_bias, "w_qkv": w_qkv, "w_attn_out": w_attn_out, "w_in": w_in, "w_down": w_down, "grad_out": grad_out}


@jax.custom_vjp
def low(v):
    return lax.optimization_barrier(v.astype(jnp.bfloat16)).astype(jnp.float32)

@jax.custom_vjp
def low_back(v):
    return v

def low_keep(v):
    return (low(v), None)

def low_pass(kept, grad):
    return (grad,)

def back_keep(v):
    return (v, None)

def back_low(kept, grad):
    return (low(grad),)
low.defvjp(low_keep, low_pass)
low_back.defvjp(back_keep, back_low)
EPSILON = 1e-05
NEGATIVE = -1e+30
PRECISE = lax.Precision.HIGHEST

def layer_norm(value, gain, bias):
    center = value - lax.optimization_barrier(jnp.mean(value, -1, keepdims=True))
    spread = lax.optimization_barrier(jnp.mean(center * center, -1, keepdims=True))
    return center * lax.rsqrt(spread + EPSILON) * gain + bias

def attend_row(queries, keys, values, segments):
    block = math.gcd(LENGTH, 512)
    count = LENGTH // block
    position = jnp.arange(LENGTH, dtype=jnp.int32)
    scale = HEAD ** (-0.5)

    def one_block(inputs):
        query_block, query_pos, query_seg = inputs
        scores = jnp.einsum('qhd,khd->hqk', query_block, keys, precision=PRECISE) * scale
        scores = low_back(scores)
        allowed = (position[None, :] <= query_pos[:, None]) & (segments[None, :] == query_seg[:, None])
        scores = jnp.where(allowed[None], scores, NEGATIVE)
        highest = lax.optimization_barrier(jnp.max(scores, -1, keepdims=True))
        weights = jnp.exp(scores - highest)
        probs = weights / lax.optimization_barrier(jnp.sum(weights, -1, keepdims=True))
        return jnp.einsum('hqk,khd->qhd', low(probs), values, precision=PRECISE)
    outputs = lax.map(jax.checkpoint(one_block), (queries.reshape(count, block, HEADS, HEAD), position.reshape(count, block), segments.reshape(count, block)))
    return outputs.reshape(LENGTH, HEADS * HEAD)

def experts(mixed, w_in, w_down, expert_ids):
    blocks = ROWS * LENGTH // SEQ_DEV
    labels = expert_ids.reshape(blocks, SEQ_DEV)
    onehot = (labels[..., None] == jnp.arange(EXPERTS, dtype=jnp.int32)).astype(jnp.int32)
    rank = jnp.cumsum(onehot, 1) - onehot
    slot = lax.optimization_barrier(jnp.sum(rank * onehot, -1))
    target = ((labels * blocks + jnp.arange(blocks, dtype=jnp.int32)[:, None]) * MOST + slot).reshape(-1)
    buffer = jnp.zeros((EXPERTS * blocks * MOST, D), jnp.float32).at[target].set(mixed.reshape(-1, D))
    buffer = buffer.reshape(EXPERTS, blocks * MOST, D)
    inner = low_back(jnp.einsum('end,edf->enf', buffer, w_in, precision=PRECISE))
    active = low(jax.nn.gelu(inner))
    result = low(low_back(jnp.einsum('enf,efd->end', active, w_down, precision=PRECISE)))
    return result.reshape(-1, D)[target].reshape(ROWS, LENGTH, D)

def forward(block_input, gain_one, bias_one, gain_two, bias_two, w_qkv, w_attn_out, w_in, w_down, segment_ids, expert_ids):
    normed = low(layer_norm(block_input, gain_one, bias_one))
    projected = low(low_back(jnp.einsum('rld,de->rle', normed, w_qkv, precision=PRECISE)))
    shape = (ROWS, LENGTH, HEADS, HEAD)
    queries = projected[..., :D].reshape(shape)
    keys = projected[..., D:2 * D].reshape(shape)
    values = projected[..., 2 * D:].reshape(shape)

    def row_step(carry, inputs):
        return (carry, attend_row(*inputs))
    _, attended = lax.scan(row_step, jnp.zeros((), jnp.float32), (queries, keys, values, segment_ids))
    attended = low(low_back(attended))
    branch = low_back(jnp.einsum('rld,de->rle', attended, w_attn_out, precision=PRECISE))
    middle = block_input + branch
    mixed = low(low_back(layer_norm(middle, gain_two, bias_two)))
    return middle + experts(mixed, w_in, w_down, expert_ids)

def reference(block_input, segment_ids, expert_ids, ln1_gain, ln1_bias, ln2_gain, ln2_bias, w_qkv, w_attn_out, w_in, w_down, grad_out):
    labels = expert_ids[..., 0]
    inputs = (block_input, ln1_gain, ln1_bias, ln2_gain, ln2_bias, w_qkv.astype(jnp.float32), w_attn_out.astype(jnp.float32), w_in.astype(jnp.float32), w_down.astype(jnp.float32))

    def closed(*params):
        return forward(*params, segment_ids, labels)
    block_output, pullback = jax.vjp(closed, *inputs)
    grads = pullback(grad_out)
    counts = lax.optimization_barrier(jnp.sum((labels[..., None] == jnp.arange(EXPERTS, dtype=jnp.int32)).astype(jnp.float32), (0, 1)))
    load = counts * (EXPERTS / (ROWS * LENGTH))
    return (block_output, grads[0], grads[5], grads[6], grads[1], grads[2], grads[3], grads[4], grads[7], grads[8], load)
```

```python
import functools
import math

import jax
import jax.numpy as jnp
from jax import lax
from jax.experimental import pallas as pl
from jax.experimental.pallas import tpu as pltpu
from jax.sharding import PartitionSpec as P

HEADS = 12
HEAD = 64
MOST = 48
PAIR = 2 * HEAD
EPSILON = 1e-05
NEGATIVE = -1e30
LOW = jnp.bfloat16
FULL = jnp.float32
VMEM_LIMIT = 60 * 1024 * 1024
NN = (((1,), (0,)), ((), ()))
NT = (((1,), (1,)), ((), ()))
TN = (((0,), (0,)), ((), ()))


def dot(a, b, dims=NN):
    return lax.dot_general(a, b, dims, preferred_element_type=FULL)


def spans(count, unroll, body):
    if unroll:
        for index in range(count):
            body(index)
    else:

        def step(index, carry):
            body(index)
            return carry

        lax.fori_loop(0, count, step, 0)


def chain(first, last, unroll, body, carry):
    if unroll:
        for index in range(first, last):
            carry = body(index, carry)
        return carry
    return lax.fori_loop(first, last, body, carry)


def tile_mask(scores, low_row, key_first, query_first, diagonal):
    key_pos = key_first + lax.broadcasted_iota(jnp.int32, scores.shape, 0)
    allowed = key_pos >= low_row
    if diagonal:
        query_pos = query_first + lax.broadcasted_iota(jnp.int32, scores.shape, 1)
        allowed = allowed & (key_pos <= query_pos)
    return allowed


def head_lanes(value, head):
    lane = lax.broadcasted_iota(jnp.int32, value.shape, 1)
    return jnp.where((lane // HEAD) == head, value, jnp.zeros_like(value))


def attend_kernel(
    block, unroll, own_ref, x_ref, wq_ref, wk_ref, wv_ref, low_ref,
    q_ref, k_ref, v_ref, o_ref, ot_ref, log_ref, vt_ref,
):
    length = x_ref.shape[0]
    count = length // block

    def project(index):
        rows = pl.ds(index * block, block)
        x = x_ref[rows, :]
        q_ref[rows, :] = (dot(x, wq_ref[...]).astype(LOW) * LOW(HEAD**-0.5)).astype(LOW)
        k_ref[rows, :] = dot(x, wk_ref[...]).astype(LOW)
        v = dot(x, wv_ref[...]).astype(LOW)
        v_ref[rows, :] = v
        vt_ref[:, rows] = v.T

    spans(count, unroll, project)

    def one_block(qi):
        rows = pl.ds(qi * block, block)
        low_row = low_ref[:, rows]
        q = q_ref[rows, :]
        done = []
        for head in range(2):
            qm = head_lanes(q, head)
            part = pl.ds(head * HEAD, HEAD)

            def tile(kj, state, diagonal):
                keys = pl.ds(kj * block, block)
                scores = dot(k_ref[keys, :], qm, NT)
                allowed = tile_mask(scores, low_row, kj * block, qi * block, diagonal)
                scores = jnp.where(allowed, scores, NEGATIVE)
                high = jnp.max(scores, 0, keepdims=True)
                if state is not None:
                    high = jnp.maximum(high, state[0])
                weights = jnp.exp(scores - high)
                total = jnp.sum(weights, 0, keepdims=True)
                summed = dot(vt_ref[part, keys], weights.astype(LOW))
                if state is not None:
                    fade = jnp.exp(state[0] - high)
                    total = total + state[1] * fade
                    summed = summed + state[2] * fade
                return high, total, summed

            state = tile(qi, None, True)
            high, total, summed = chain(
                0, qi, unroll, lambda kj, carry: tile(kj, carry, False), state
            )
            log_ref[0, pl.ds(head, 1), rows] = high + jnp.log(total)
            done.append(summed / total)
        both = jnp.concatenate(done, 0)
        ot_ref[:, rows] = both
        o_ref[rows, :] = both.T.astype(LOW)

    spans(count, unroll, one_block)


def attend_back_kernel(
    block, unroll, own_ref, x_ref, wq_ref, wk_ref, wv_ref, low_ref,
    q_ref, k_ref, v_ref, g_ref, ot_ref, log_ref,
    gx_ref, gw_ref, kt_ref, delta_ref, dqt_ref, dk_ref, dv_ref, sum_ref,
):
    length = x_ref.shape[0]
    count = length // block
    width = x_ref.shape[1]
    scale = HEAD**-0.5
    pair = pl.program_id(0)

    def prepare(index):
        rows = pl.ds(index * block, block)
        kt_ref[:, rows] = k_ref[rows, :].T
        product = g_ref[rows, :].astype(FULL).T * ot_ref[:, rows]
        for head in range(2):
            part = product[head * HEAD : (head + 1) * HEAD]
            delta_ref[pl.ds(head, 1), rows] = jnp.sum(part, 0, keepdims=True)
        dqt_ref[:, rows] = jnp.zeros((PAIR, block), FULL)

    spans(count, unroll, prepare)

    def one_block(kj):
        keys = pl.ds(kj * block, block)
        k = k_ref[keys, :]
        v = v_ref[keys, :]

        def tile(qi, carry, diagonal):
            grad_k, grad_v = carry
            rows = pl.ds(qi * block, block)
            q = q_ref[rows, :]
            g = g_ref[rows, :]
            low_row = low_ref[:, rows]
            for head in range(2):
                qm = head_lanes(q, head)
                gm = head_lanes(g, head)
                part = pl.ds(head * HEAD, HEAD)
                scores = dot(k, qm, NT)
                allowed = tile_mask(scores, low_row, kj * block, qi * block, diagonal)
                probs = jnp.exp(scores - log_ref[0, pl.ds(head, 1), rows])
                probs = jnp.where(allowed, probs, 0.0)
                grad_probs = dot(v, gm, NT)
                grad_scores = (probs * (grad_probs - delta_ref[pl.ds(head, 1), rows])).astype(LOW)
                grad_v = grad_v + dot(probs.astype(LOW), gm)
                grad_k = grad_k + dot(grad_scores, qm)
                dqt_ref[part, rows] += dot(kt_ref[part, keys], grad_scores)
            return grad_k, grad_v

        zero = jnp.zeros((block, PAIR), FULL)
        carry = tile(kj, (zero, zero), True)
        grad_k, grad_v = chain(
            kj + 1, count, unroll, lambda qi, carry: tile(qi, carry, False), carry
        )
        dk_ref[keys, :] = grad_k.astype(LOW)
        dv_ref[keys, :] = grad_v.astype(LOW)

    spans(count, unroll, one_block)

    @pl.when(pair == 0)
    def _():
        sum_ref[...] = jnp.zeros_like(sum_ref)

    gw_ref[...] = jnp.zeros_like(gw_ref)

    def spread(index):
        rows = pl.ds(index * block, block)
        dq = (dqt_ref[:, rows] * scale).T.astype(LOW)
        dk = dk_ref[rows, :]
        dv = dv_ref[rows, :]
        total = dot(dq, wq_ref[...], NT) + dot(dk, wk_ref[...], NT) + dot(dv, wv_ref[...], NT)
        sum_ref[rows, :] += total
        x = x_ref[rows, :]
        gw_ref[0] += dot(x, dq, TN)
        gw_ref[1] += dot(x, dk, TN)
        gw_ref[2] += dot(x, dv, TN)

    spans(count, unroll, spread)

    @pl.when(pair == pl.num_programs(0) - 1)
    def _():
        gx_ref[...] = sum_ref[...].astype(LOW)


def attention_specs(length, width, pairs, all_pairs):
    whole = lambda: pl.BlockSpec((length, width), lambda p, own: (0, 0))
    weight = lambda which: pl.BlockSpec(
        (width, PAIR), lambda p, own: (0, which * all_pairs + own[0] * pairs + p)
    )
    low = pl.BlockSpec((1, length), lambda p, own: (0, 0))
    columns = lambda: pl.BlockSpec((length, PAIR), lambda p, own: (0, p))
    across = pl.BlockSpec((PAIR, length), lambda p, own: (p, 0))
    logs = pl.BlockSpec((1, 2, length), lambda p, own: (p, 0, 0))
    return whole, weight, low, columns, across, logs


def attend(own, x, weights, low, pairs, all_pairs):
    length, width = x.shape
    block = math.gcd(length, 256)
    unroll = length // block <= 4
    whole, weight, lows, columns, across, logs = attention_specs(length, width, pairs, all_pairs)
    shape = jax.ShapeDtypeStruct
    return pl.pallas_call(
        functools.partial(attend_kernel, block, unroll),
        grid_spec=pltpu.PrefetchScalarGridSpec(
            num_scalar_prefetch=1,
            grid=(pairs,),
            in_specs=[whole(), weight(0), weight(1), weight(2), lows],
            out_specs=[columns(), columns(), columns(), columns(), across, logs],
            scratch_shapes=[pltpu.VMEM((PAIR, length), LOW)],
        ),
        out_shape=[shape((length, pairs * PAIR), LOW)] * 4
        + [shape((pairs * PAIR, length), FULL), shape((pairs, 2, length), FULL)],
        compiler_params=pltpu.CompilerParams(vmem_limit_bytes=VMEM_LIMIT),
        cost_estimate=pl.CostEstimate(
            flops=2 * length * width * 3 * pairs * PAIR + 8 * length * length * pairs * PAIR,
            bytes_accessed=2 * length * width + 12 * length * pairs * PAIR,
            transcendentals=length * length * pairs,
        ),
        name="attend",
    )(own, x, weights, weights, weights, low)


def attend_back(own, x, weights, low, q, k, v, g, ot, logs_in, pairs, all_pairs):
    length, width = x.shape
    block = math.gcd(length, 256)
    unroll = length // block <= 4
    whole, weight, lows, columns, across, logs = attention_specs(length, width, pairs, all_pairs)
    shape = jax.ShapeDtypeStruct
    return pl.pallas_call(
        functools.partial(attend_back_kernel, block, unroll),
        grid_spec=pltpu.PrefetchScalarGridSpec(
            num_scalar_prefetch=1,
            grid=(pairs,),
            in_specs=[whole(), weight(0), weight(1), weight(2), lows]
            + [columns(), columns(), columns(), columns(), across, logs],
            out_specs=[whole(), pl.BlockSpec((3, width, PAIR), lambda p, own: (0, 0, p))],
            scratch_shapes=[
                pltpu.VMEM((PAIR, length), LOW),
                pltpu.VMEM((2, length), FULL),
                pltpu.VMEM((PAIR, length), FULL),
                pltpu.VMEM((length, PAIR), LOW),
                pltpu.VMEM((length, PAIR), LOW),
                pltpu.VMEM((length, width), FULL),
            ],
        ),
        out_shape=[shape((length, width), LOW), shape((3, width, pairs * PAIR), FULL)],
        compiler_params=pltpu.CompilerParams(vmem_limit_bytes=VMEM_LIMIT),
        cost_estimate=pl.CostEstimate(
            flops=4 * length * width * 3 * pairs * PAIR + 20 * length * length * pairs * PAIR,
            bytes_accessed=4 * length * width + 24 * length * pairs * PAIR,
            transcendentals=length * length * pairs,
        ),
        name="attend_back",
    )(own, x, weights, weights, weights, low, q, k, v, g, ot, logs_in)


GELU_SCALE = math.sqrt(2.0 / math.pi)
GELU_CUBE = 0.044715


def expert_kernel(
    x_ref, g_ref, up_ref, down_ref, y_ref, gx_ref, gup_ref, gdown_ref, y_sum, gx_sum
):
    step = pl.program_id(0)
    x = x_ref[...]
    g = g_ref[...]
    inner = dot(x, up_ref[...])
    square = inner * inner
    curve = jnp.tanh(GELU_SCALE * inner * (1.0 + GELU_CUBE * square))
    half = 0.5 + 0.5 * curve
    active = (inner * half).astype(LOW)
    slope = half + (0.5 * GELU_SCALE) * inner * (1.0 - curve * curve) * (
        1.0 + (3.0 * GELU_CUBE) * square
    )
    grad_inner = (dot(g, down_ref[...], NT) * slope).astype(LOW)
    gdown_ref[...] = dot(active, g, TN).astype(LOW)
    gup_ref[...] = dot(x, grad_inner, TN).astype(LOW)
    y = dot(active, down_ref[...])
    gx = dot(grad_inner, up_ref[...], NT)

    @pl.when(step == 0)
    def _():
        y_sum[...] = y
        gx_sum[...] = gx

    @pl.when(step > 0)
    def _():
        y_sum[...] += y
        gx_sum[...] += gx

    @pl.when(step == pl.num_programs(0) - 1)
    def _():
        y_ref[...] = y_sum[...].astype(LOW)
        gx_ref[...] = gx_sum[...].astype(LOW)


def expert(x, g, up, down):
    slots, width = x.shape
    hidden = up.shape[1]
    block = math.gcd(hidden, 512)
    rows = lambda: pl.BlockSpec((slots, width), lambda f: (0, 0))
    ups = lambda: pl.BlockSpec((width, block), lambda f: (0, f))
    downs = lambda: pl.BlockSpec((block, width), lambda f: (f, 0))
    shape = jax.ShapeDtypeStruct
    return pl.pallas_call(
        expert_kernel,
        grid=(hidden // block,),
        in_specs=[rows(), rows(), ups(), downs()],
        out_specs=[rows(), rows(), ups(), downs()],
        out_shape=[shape((slots, width), LOW)] * 2
        + [shape((width, hidden), LOW), shape((hidden, width), LOW)],
        scratch_shapes=[pltpu.VMEM((slots, width), FULL)] * 2,
        compiler_params=pltpu.CompilerParams(vmem_limit_bytes=VMEM_LIMIT),
        cost_estimate=pl.CostEstimate(
            flops=12 * slots * width * hidden,
            bytes_accessed=8 * width * hidden + 8 * slots * width,
            transcendentals=slots * hidden,
        ),
        name="expert",
    )(x, g, up, down)


def standard(value):
    center = value - jnp.mean(value, -1, keepdims=True)
    spread = jnp.mean(center * center, -1, keepdims=True)
    inverse = lax.rsqrt(spread + EPSILON)
    return center * inverse, inverse


def standard_back(grad, gain, unit, inverse):
    u = grad * gain
    lean = jnp.mean(u * unit, -1, keepdims=True)
    back = (u - jnp.mean(u, -1, keepdims=True) - unit * lean) * inverse
    return back, jnp.sum(grad * unit, 0), jnp.sum(grad, 0)


def per_device(
    block_input, segment_ids, expert_ids, ln1_gain, ln1_bias, ln2_gain, ln2_bias,
    w_qkv, w_attn_out, w_in, w_down, grad_out,
):
    rows, local, width = block_input.shape
    seq = lax.axis_size("seq")
    experts = lax.axis_size("ex")
    team = seq // rows
    length = seq * local
    owned = rows * local
    pairs = -(-HEADS // (2 * team))
    share = pairs * PAIR
    all_pairs = pairs * team
    padded = all_pairs * PAIR
    place = lax.axis_index("seq")
    row, member = place // team, place % team
    across_rows = [[r * team + g for r in range(rows)] for g in range(team)]
    in_row = [[r * team + g for g in range(team)] for r in range(rows)]

    def swap_rows(value):
        return lax.all_to_all(value, "seq", 0, 0, tiled=True, axis_index_groups=across_rows)

    def swap_team(value):
        return lax.all_to_all(value, "seq", 0, 0, tiled=True, axis_index_groups=in_row)

    def swap_experts(value):
        return lax.all_to_all(value, "ex", 0, 0, tiled=True)

    center = block_input - jnp.mean(block_input, -1, keepdims=True)
    residual = swap_rows(center.astype(LOW)).reshape(owned, width).astype(FULL)
    chosen = swap_rows(expert_ids[..., 0])
    grad_low = swap_rows(grad_out.astype(LOW))

    segments = lax.dynamic_slice_in_dim(segment_ids, row, 1, 0)[0]
    lows = jnp.sum((segments[:, None] < segments[None, :]).astype(jnp.int32), 0)[None, :]

    weights = w_qkv
    out_weights = w_attn_out
    if padded != width:
        weights = jnp.pad(
            w_qkv.reshape(width, 3, width), ((0, 0), (0, 0), (0, padded - width))
        ).reshape(width, 3 * padded)

    unit_one, inverse_one = standard(residual)
    normed_one = (unit_one * ln1_gain + ln1_bias).astype(LOW)
    gathered = swap_team(
        jnp.broadcast_to(normed_one[None], (team, owned, width))
    ).reshape(team, rows, local, width)
    full = jnp.swapaxes(gathered, 0, 1).reshape(length, width)

    own = member.reshape(1).astype(jnp.int32)
    q, k, v, o, ot, logs = attend(own, full, weights, lows, pairs, all_pairs)

    def to_owners(value):
        parts = value.reshape(rows, team, local, value.shape[-1])
        parts = jnp.swapaxes(parts, 0, 1)
        return swap_team(parts).reshape(team, owned, value.shape[-1])

    attended = jnp.swapaxes(to_owners(o), 0, 1).reshape(owned, padded)[:, :width]
    branch = dot(attended, out_weights)
    middle = residual + branch
    unit_two, inverse_two = standard(middle)
    normed_two = (unit_two * ln2_gain + ln2_bias).astype(LOW)

    onehot = (chosen[..., None] == jnp.arange(experts, dtype=jnp.int32)).astype(jnp.int32)
    rank = jnp.cumsum(onehot, 1) - onehot
    target = chosen * MOST + jnp.sum(rank * onehot, -1)
    route = (
        (target[:, None, :] == jnp.arange(experts * MOST, dtype=jnp.int32)[None, :, None])
        .astype(LOW)
        .reshape(rows, experts, MOST, local)
    )
    counts = jnp.sum(onehot.astype(FULL), (0, 1))

    def dispatch(value):
        placed = jnp.einsum(
            "remt,rtd->ermd", route, value.reshape(rows, local, width), preferred_element_type=FULL
        )
        return swap_experts(placed.astype(LOW).reshape(experts, rows * MOST, width)).reshape(
            experts * rows * MOST, width
        )

    def collect(value):
        returned = swap_experts(value.reshape(experts, rows * MOST, width))
        return jnp.einsum(
            "remt,ermd->rtd",
            route,
            returned.reshape(experts, rows, MOST, width),
            preferred_element_type=FULL,
        ).reshape(owned, width)

    grad_arrived = dispatch(grad_low)
    arrived = dispatch(normed_two)
    produced, grad_rows, grad_up, grad_down = expert(arrived, grad_arrived, w_in[0], w_down[0])

    grad_normed_two = collect(grad_rows)
    back_two, grad_gain_two, grad_bias_two = standard_back(
        grad_normed_two, ln2_gain, unit_two, inverse_two
    )
    grad_branch = (back_two + grad_low.reshape(owned, width).astype(FULL)).astype(LOW)
    grad_attended = dot(grad_branch, out_weights, NT).astype(LOW)
    if padded != width:
        grad_attended = jnp.pad(grad_attended, ((0, 0), (0, padded - width)))
    parted = jnp.swapaxes(grad_attended.reshape(owned, team, share), 0, 1)
    grad_heads = jnp.swapaxes(swap_team(parted).reshape(team, rows, local, share), 0, 1)
    grad_full, grad_weights = attend_back(
        own, full, weights, lows, q, k, v, grad_heads.reshape(length, share), ot, logs,
        pairs, all_pairs,
    )

    expert_part = collect(produced)
    change = swap_rows((branch + expert_part).astype(LOW).reshape(rows, local, width))
    block_output = block_input + change.astype(FULL)

    grad_attn_out = dot(attended, grad_branch, TN)

    grad_normed_one = jnp.sum(to_owners(grad_full).astype(FULL), 0)
    back_one, grad_gain_one, grad_bias_one = standard_back(
        grad_normed_one, ln1_gain, unit_one, inverse_one
    )
    grad_change = swap_rows((back_two + back_one).astype(LOW).reshape(rows, local, width))
    grad_input = grad_out + grad_change.astype(FULL)

    cut = width // (experts * rows)
    parts = grad_weights.astype(LOW).reshape(3, experts, rows, cut, share)
    parts = jnp.transpose(parts, (1, 2, 0, 3, 4))
    parts = jnp.sum(swap_experts(parts).astype(FULL), 0)
    parts = jnp.sum(swap_rows(parts.astype(LOW)).astype(FULL), 0).astype(LOW)
    parts = swap_rows(jnp.broadcast_to(parts[None], (rows,) + parts.shape))
    parts = swap_team(jnp.broadcast_to(parts[None], (team,) + parts.shape))
    parts = swap_experts(jnp.broadcast_to(parts[None], (experts,) + parts.shape))
    parts = parts.reshape(experts, team, rows, 3, cut, share)
    grad_qkv = jnp.transpose(parts, (0, 2, 4, 3, 1, 5)).reshape(width, 3, padded)[..., :width]
    grad_qkv = grad_qkv.reshape(width, 3 * width).astype(FULL)

    grad_attn_out = lax.psum(grad_attn_out.astype(LOW), ("seq", "ex")).astype(FULL)
    small = jnp.stack([grad_gain_one, grad_bias_one, grad_gain_two, grad_bias_two])
    small, counts = lax.psum((small, counts), ("seq", "ex"))
    expert_grads = (
        lax.psum(grad_up, "seq").astype(FULL),
        lax.psum(grad_down, "seq").astype(FULL),
    )
    load = counts * (experts / (rows * length * experts))
    return (
        block_output, grad_input, grad_qkv, grad_attn_out, small[0], small[1], small[2], small[3],
        expert_grads[0][None], expert_grads[1][None], load,
    )


def solution(mesh):
    tokens = P("ex", "seq", None)
    expert_axis = P("ex", None, None)
    return jax.shard_map(
        per_device,
        mesh=mesh,
        in_specs=(
            tokens, P("ex", None), tokens, P(), P(), P(), P(), P(), P(),
            expert_axis, expert_axis, tokens,
        ),
        out_specs=(
            tokens, tokens, P(), P(), P(), P(), P(), P(), expert_axis, expert_axis, P(),
        ),
        check_vma=False,
    )
```

```python
import functools
import math

import jax
import jax.numpy as jnp
from jax import lax
from jax.experimental import pallas as pl
from jax.experimental.pallas import tpu as pltpu
from jax.sharding import PartitionSpec as P

HEADS = 12
HEAD = 64
MOST = 48
PAIR = 2 * HEAD
EPSILON = 1e-05
NEGATIVE = -1e30
LOW = jnp.bfloat16
FULL = jnp.float32
VMEM_LIMIT = 60 * 1024 * 1024
NN = (((1,), (0,)), ((), ()))
NT = (((1,), (1,)), ((), ()))
TN = (((0,), (0,)), ((), ()))


def dot(a, b, dims=NN):
    return lax.dot_general(a, b, dims, preferred_element_type=FULL)


def loop(first, last, unroll, body, carry):
    if unroll:
        for index in range(first, last):
            carry = body(index, carry)
        return carry
    return lax.fori_loop(first, last, body, carry)


def each(count, unroll, body):
    def step(index, carry):
        body(index)
        return carry

    loop(0, count, unroll, step, 0)


def tile_mask(shape, low_row, key_first, query_first, diagonal):
    key_pos = key_first + lax.broadcasted_iota(jnp.int32, shape, 0)
    allowed = key_pos >= low_row
    if diagonal:
        query_pos = query_first + lax.broadcasted_iota(jnp.int32, shape, 1)
        allowed = allowed & (key_pos <= query_pos)
    return allowed


def head_lanes(value, head):
    lane = lax.broadcasted_iota(jnp.int32, value.shape, 1)
    return jnp.where((lane // HEAD) == head, value, jnp.zeros_like(value))


def place_of(own_ref, j, k, team, rows, local):
    row = lax.rem(own_ref[0] + (rows - k), rows)
    member = lax.rem(own_ref[1] + (team + j) % team, team)
    return pl.ds(pl.multiple_of((row * team + member) * local, local), local)


def standard(value):
    center = value - jnp.mean(value, -1, keepdims=True)
    spread = jnp.mean(center * center, -1, keepdims=True)
    inverse = lax.rsqrt(spread + EPSILON)
    return center * inverse, inverse


def standard_back(grad, gain, unit, inverse):
    u = grad * gain
    lean = jnp.mean(u * unit, -1, keepdims=True)
    back = (u - jnp.mean(u, -1, keepdims=True) - unit * lean) * inverse
    return back, jnp.sum(grad * unit, 0), jnp.sum(grad, 0)


def attend_kernel(team, rows, local, block, unroll, own_ref, *refs):
    pieces, refs = refs[: team * rows], refs[team * rows :]
    gain_ref, bias_ref, wq_ref, wk_ref, wv_ref, low_ref = refs[:6]
    x_ref, q_ref, k_ref, v_ref, ot_ref, log_ref = refs[6:12]
    o_refs = refs[12 : 12 + team]
    vt_ref, o_ref = refs[12 + team :]
    length = x_ref.shape[0]
    count = length // block

    @pl.when(pl.program_id(0) == 0)
    def _():
        for j in range(team):
            for k in range(rows):
                unit, _ = standard(pieces[j * rows + k][...].astype(FULL))
                normed = unit * gain_ref[...] + bias_ref[...]
                x_ref[place_of(own_ref, -j, k, team, rows, local), :] = normed.astype(LOW)

    def project(index):
        span = pl.ds(index * block, block)
        x = x_ref[span, :]
        q_ref[span, :] = (dot(x, wq_ref[...]).astype(LOW) * LOW(HEAD**-0.5)).astype(LOW)
        k_ref[span, :] = dot(x, wk_ref[...]).astype(LOW)
        v = dot(x, wv_ref[...]).astype(LOW)
        v_ref[span, :] = v
        vt_ref[:, span] = v.T

    each(count, unroll, project)

    def one_block(qi):
        span = pl.ds(qi * block, block)
        low_row = low_ref[:, span]
        q = q_ref[span, :]
        masked = [head_lanes(q, head) for head in range(2)]

        def tile(kj, state, diagonal):
            keys = pl.ds(kj * block, block)
            k = k_ref[keys, :]
            allowed = tile_mask((block, block), low_row, kj * block, qi * block, diagonal)
            after = []
            for head in range(2):
                scores = jnp.where(allowed, dot(k, masked[head], NT), NEGATIVE)
                high = jnp.max(scores, 0, keepdims=True)
                if state is not None:
                    high = jnp.maximum(high, state[head][0])
                weights = jnp.exp(scores - high)
                total = jnp.sum(weights, 0, keepdims=True)
                summed = dot(vt_ref[pl.ds(head * HEAD, HEAD), keys], weights.astype(LOW))
                if state is not None:
                    fade = jnp.exp(state[head][0] - high)
                    total = total + state[head][1] * fade
                    summed = summed + state[head][2] * fade
                after.append((high, total, summed))
            return tuple(after)

        state = loop(
            0, qi, unroll, lambda kj, carry: tile(kj, carry, False), tile(qi, None, True)
        )
        done = []
        for head in range(2):
            high, total, summed = state[head]
            log_ref[0, pl.ds(head, 1), span] = high + jnp.log(total)
            done.append(summed / total)
        both = jnp.concatenate(done, 0)
        ot_ref[:, span] = both
        o_ref[span, :] = both.T.astype(LOW)

    each(count, unroll, one_block)
    for j in range(team):
        for k in range(rows):
            o_refs[j][k] = o_ref[place_of(own_ref, j, k, team, rows, local), :]


def attend_back_kernel(team, rows, local, block, unroll, own_ref, *refs):
    pieces, refs = refs[:team], refs[team:]
    x_ref, wq_ref, wk_ref, wv_ref, wo_ref, low_ref = refs[:6]
    q_ref, k_ref, v_ref, ot_ref, log_ref, gw_ref = refs[6:12]
    gx_refs = refs[12 : 12 + team]
    b_ref, g_ref, kt_ref, delta_ref, dqt_ref, d_ref, sum_ref = refs[12 + team :]
    length, width = x_ref.shape
    count = length // block
    scale = HEAD**-0.5
    pair = pl.program_id(0)

    @pl.when(pair == 0)
    def _():
        for j in range(team):
            for k in range(rows):
                b_ref[place_of(own_ref, -j, k, team, rows, local), :] = pieces[j][k]
        sum_ref[...] = jnp.zeros_like(sum_ref)

    def prepare(index):
        span = pl.ds(index * block, block)
        kt_ref[:, span] = k_ref[span, :].T
        g = dot(b_ref[span, :], wo_ref[...], NT).astype(LOW)
        g_ref[span, :] = g
        product = g.astype(FULL).T * ot_ref[:, span]
        for head in range(2):
            part = product[head * HEAD : (head + 1) * HEAD]
            delta_ref[pl.ds(head, 1), span] = jnp.sum(part, 0, keepdims=True)
        dqt_ref[:, span] = jnp.zeros((PAIR, block), FULL)

    each(count, unroll, prepare)

    def one_block(kj):
        keys = pl.ds(kj * block, block)
        k = k_ref[keys, :]
        v = v_ref[keys, :]

        def tile(qi, carry, diagonal):
            grad_k, grad_v = carry
            span = pl.ds(qi * block, block)
            q = q_ref[span, :]
            g = g_ref[span, :]
            allowed = tile_mask(
                (block, block), low_ref[:, span], kj * block, qi * block, diagonal
            )
            for head in range(2):
                qm = head_lanes(q, head)
                gm = head_lanes(g, head)
                part = pl.ds(head * HEAD, HEAD)
                probs = jnp.exp(dot(k, qm, NT) - log_ref[0, pl.ds(head, 1), span])
                probs = jnp.where(allowed, probs, 0.0)
                grad_probs = dot(v, gm, NT)
                grad_scores = (probs * (grad_probs - delta_ref[pl.ds(head, 1), span])).astype(LOW)
                grad_v = grad_v + dot(probs.astype(LOW), gm)
                grad_k = grad_k + dot(grad_scores, qm)
                dqt_ref[part, span] += dot(kt_ref[part, keys], grad_scores)
            return grad_k, grad_v

        zero = jnp.zeros((block, PAIR), FULL)
        grad_k, grad_v = loop(
            kj + 1,
            count,
            unroll,
            lambda qi, carry: tile(qi, carry, False),
            tile(kj, (zero, zero), True),
        )
        d_ref[keys, PAIR : 2 * PAIR] = grad_k.astype(LOW)
        d_ref[keys, 2 * PAIR :] = grad_v.astype(LOW)

    each(count, unroll, one_block)

    weight = jnp.concatenate([wq_ref[...], wk_ref[...], wv_ref[...]], 1)

    def spread(index):
        span = pl.ds(index * block, block)
        d_ref[span, :PAIR] = (dqt_ref[:, span] * scale).T.astype(LOW)
        sum_ref[span, :] += dot(d_ref[span, :], weight, NT)

    each(count, unroll, spread)

    grads = dot(x_ref[...], d_ref[...], TN)
    for which in range(3):
        gw_ref[which] = grads[:, which * PAIR : (which + 1) * PAIR].astype(LOW)
    gw_ref[3] = dot(ot_ref[...].astype(LOW), b_ref[...]).T.astype(LOW)

    @pl.when(pair == pl.num_programs(0) - 1)
    def _():
        for j in range(team):
            for k in range(rows):
                gx_refs[j][k] = sum_ref[place_of(own_ref, j, k, team, rows, local), :].astype(LOW)


def fixed(*shape):
    return pl.BlockSpec(shape, lambda p, own: (0,) * len(shape), pipeline_mode=pl.Buffered(1))


def attention_specs(length, width, pairs, all_pairs):
    weight = lambda which: pl.BlockSpec(
        (width, PAIR), lambda p, own: (0, which * all_pairs + own[1] * pairs + p)
    )
    columns = lambda: pl.BlockSpec((length, PAIR), lambda p, own: (0, p))
    across = pl.BlockSpec((PAIR, length), lambda p, own: (p, 0))
    logs = pl.BlockSpec((1, 2, length), lambda p, own: (p, 0, 0))
    return weight, columns, across, logs


def attend(own, pieces, gain, bias, weights, low, team, rows, pairs):
    local, width = pieces[0].shape
    length = team * rows * local
    share = pairs * PAIR
    block = math.gcd(length, 256)
    unroll = length // block <= 4
    weight, columns, across, logs = attention_specs(length, width, pairs, pairs * team)
    shape = jax.ShapeDtypeStruct
    return pl.pallas_call(
        functools.partial(attend_kernel, team, rows, local, block, unroll),
        grid_spec=pltpu.PrefetchScalarGridSpec(
            num_scalar_prefetch=1,
            grid=(pairs,),
            in_specs=[fixed(local, width)] * len(pieces)
            + [fixed(1, width)] * 2
            + [weight(0), weight(1), weight(2), fixed(1, length)],
            out_specs=[pl.BlockSpec((length, width), lambda p, own: (0, 0))]
            + [columns(), columns(), columns(), across, logs]
            + [pl.BlockSpec((rows, local, PAIR), lambda p, own: (0, 0, p))] * team,
            scratch_shapes=[pltpu.VMEM((PAIR, length), LOW), pltpu.VMEM((length, PAIR), LOW)],
        ),
        out_shape=[shape((length, width), LOW)]
        + [shape((length, share), LOW)] * 3
        + [shape((share, length), FULL), shape((pairs, 2, length), FULL)]
        + [shape((rows, local, share), LOW)] * team,
        compiler_params=pltpu.CompilerParams(vmem_limit_bytes=VMEM_LIMIT),
        cost_estimate=pl.CostEstimate(
            flops=2 * length * width * 3 * share + 8 * length * length * share,
            bytes_accessed=4 * length * width + 12 * length * share,
            transcendentals=length * length * pairs,
        ),
        name="attend",
    )(own, *pieces, gain[None], bias[None], weights, weights, weights, low)


def attend_back(own, pieces, x, weights, out_weights, low, q, k, v, ot, logs_in, team, rows, pairs):
    length, width = x.shape
    local = length // (team * rows)
    share = pairs * PAIR
    block = math.gcd(length, 256)
    unroll = length // block <= 4
    weight, columns, across, logs = attention_specs(length, width, pairs, pairs * team)
    shape = jax.ShapeDtypeStruct
    out = pl.BlockSpec((rows, local, width), lambda p, own: (0, 0, 0))
    results = pl.pallas_call(
        functools.partial(attend_back_kernel, team, rows, local, block, unroll),
        grid_spec=pltpu.PrefetchScalarGridSpec(
            num_scalar_prefetch=1,
            grid=(pairs,),
            in_specs=[fixed(rows, local, width)] * team
            + [fixed(length, width), weight(0), weight(1), weight(2)]
            + [pl.BlockSpec((PAIR, width), lambda p, own: (own[1] * pairs + p, 0))]
            + [fixed(1, length), columns(), columns(), columns(), across, logs],
            out_specs=[pl.BlockSpec((4, width, PAIR), lambda p, own: (0, 0, p))] + [out] * team,
            scratch_shapes=[
                pltpu.VMEM((length, width), LOW),
                pltpu.VMEM((length, PAIR), LOW),
                pltpu.VMEM((PAIR, length), LOW),
                pltpu.VMEM((2, length), FULL),
                pltpu.VMEM((PAIR, length), FULL),
                pltpu.VMEM((length, 3 * PAIR), LOW),
                pltpu.VMEM((length, width), FULL),
            ],
        ),
        out_shape=[shape((4, width, share), LOW)] + [shape((rows, local, width), LOW)] * team,
        compiler_params=pltpu.CompilerParams(vmem_limit_bytes=VMEM_LIMIT),
        cost_estimate=pl.CostEstimate(
            flops=4 * length * width * 4 * share + 20 * length * length * share,
            bytes_accessed=6 * length * width + 24 * length * share,
            transcendentals=length * length * pairs,
        ),
        name="attend_back",
    )(own, *pieces, x, weights, weights, weights, out_weights, low, q, k, v, ot, logs_in)
    return results[0], results[1:]


GELU_SCALE = math.sqrt(2.0 / math.pi)
GELU_CUBE = 0.044715


def expert_kernel(count, first, last, *refs):
    x_refs, refs = refs[:count], refs[count:]
    g_refs, refs = refs[:count], refs[count:]
    up_ref, down_ref, refs = refs[0], refs[1], refs[2:]
    if not first:
        y_in, gx_in, refs = refs[0], refs[1], refs[2:]
    gup_ref, gdown_ref, refs = refs[0], refs[1], refs[2:]
    if last:
        y_outs, refs = refs[:count], refs[count:]
        gx_outs, refs = refs[:count], refs[count:]
        y_sum, gx_sum, refs = refs[0], refs[1], refs[2:]
    else:
        y_sum, gx_sum, refs = refs[0], refs[1], refs[2:]
    x_ref, g_ref = refs
    step = pl.program_id(0)
    size = x_refs[0].shape[0]

    @pl.when(step == 0)
    def _():
        for index in range(count):
            span = pl.ds(index * size, size)
            x_ref[span, :] = x_refs[index][...]
            g_ref[span, :] = g_refs[index][...]
        if first:
            y_sum[...] = jnp.zeros_like(y_sum)
            gx_sum[...] = jnp.zeros_like(gx_sum)
        else:
            y_sum[...] = y_in[...]
            gx_sum[...] = gx_in[...]

    x = x_ref[...]
    g = g_ref[...]
    inner = dot(x, up_ref[...])
    square = inner * inner
    curve = jnp.tanh(GELU_SCALE * inner * (1.0 + GELU_CUBE * square))
    half = 0.5 + 0.5 * curve
    active = (inner * half).astype(LOW)
    slope = half + (0.5 * GELU_SCALE) * inner * (1.0 - curve * curve) * (
        1.0 + (3.0 * GELU_CUBE) * square
    )
    grad_inner = (dot(g, down_ref[...], NT) * slope).astype(LOW)
    gdown_ref[...] = dot(active, g, TN).astype(LOW)
    gup_ref[...] = dot(x, grad_inner, TN).astype(LOW)
    y_sum[...] += dot(active, down_ref[...])
    gx_sum[...] += dot(grad_inner, up_ref[...], NT)

    if last:

        @pl.when(step == pl.num_programs(0) - 1)
        def _():
            for index in range(count):
                span = pl.ds(index * size, size)
                y_outs[index][...] = y_sum[span, :].astype(LOW)
                gx_outs[index][...] = gx_sum[span, :].astype(LOW)


def expert(xs, gs, up, down, part, parts, sums):
    count = len(xs)
    size, width = xs[0].shape
    hidden = up.shape[1] // parts
    block = math.gcd(hidden, 512)
    steps = hidden // block
    first, last = part == 0, part == parts - 1
    rows = pl.BlockSpec((size, width), lambda f: (0, 0))
    whole = pl.BlockSpec((count * size, width), lambda f: (0, 0))
    shape = jax.ShapeDtypeStruct
    sum_shape = shape((count * size, width), FULL)
    in_specs = [rows] * (2 * count) + [
        pl.BlockSpec((width, block), lambda f: (0, f + part * steps)),
        pl.BlockSpec((block, width), lambda f: (f + part * steps, 0)),
    ]
    out_specs = [
        pl.BlockSpec((width, block), lambda f: (0, f)),
        pl.BlockSpec((block, width), lambda f: (f, 0)),
    ]
    out_shape = [shape((width, hidden), LOW), shape((hidden, width), LOW)]
    scratch = []
    if not first:
        in_specs += [whole] * 2
    if last:
        out_specs += [rows] * (2 * count)
        out_shape += [shape((size, width), LOW)] * (2 * count)
        scratch += [pltpu.VMEM(sum_shape.shape, FULL)] * 2
    else:
        out_specs += [whole] * 2
        out_shape += [sum_shape] * 2
    results = pl.pallas_call(
        functools.partial(expert_kernel, count, first, last),
        grid=(steps,),
        in_specs=in_specs,
        out_specs=out_specs,
        out_shape=out_shape,
        scratch_shapes=scratch + [pltpu.VMEM((count * size, width), LOW)] * 2,
        compiler_params=pltpu.CompilerParams(vmem_limit_bytes=VMEM_LIMIT),
        cost_estimate=pl.CostEstimate(
            flops=12 * count * size * width * hidden,
            bytes_accessed=8 * width * hidden + 8 * count * size * width,
            transcendentals=count * size * hidden,
        ),
        name="expert",
    )(*xs, *gs, up, down, *sums)
    return results[0], results[1], results[2:]


def add_low(a, b):
    return (a.astype(FULL) + b.astype(FULL)).astype(LOW)


def pick(value, index):
    return lax.dynamic_index_in_dim(value, index, 0, keepdims=False)


def ring_scatter(value, size, place, send):
    total = pick(value, (place + size - 1) % size)
    for step in range(size - 1):
        total = add_low(send(total), pick(value, (place + 2 * size - 2 - step) % size))
    return total


def ring_gather(value, size, place, send):
    out = jnp.zeros((size,) + value.shape, value.dtype)
    out = lax.dynamic_update_index_in_dim(out, value, place, 0)
    for step in range(size - 1):
        value = send(value)
        out = lax.dynamic_update_index_in_dim(out, value, (place + size - 1 - step) % size, 0)
    return out


def per_device(
    block_input, segment_ids, expert_ids, ln1_gain, ln1_bias, ln2_gain, ln2_bias,
    w_qkv, w_attn_out, w_in, w_down, grad_out,
):
    rows, local, width = block_input.shape
    seq = lax.axis_size("seq")
    experts = lax.axis_size("ex")
    team = seq // rows
    length = seq * local
    owned = rows * local
    pairs = -(-HEADS // (2 * team))
    share = pairs * PAIR
    padded = share * team
    place = lax.axis_index("seq")
    mine = lax.axis_index("ex")
    row, member = place // team, place % team
    slots = rows * MOST

    def row_send(value, k):
        if k % rows == 0:
            return value
        pattern = [(a * team + b, (a + k) % rows * team + b) for a in range(rows) for b in range(team)]
        return lax.ppermute(value, "seq", pattern)

    def team_send(value, j):
        if j % team == 0:
            return value
        pattern = [(a * team + b, a * team + (b + j) % team) for a in range(rows) for b in range(team)]
        return lax.ppermute(value, "seq", pattern)

    def swap(value, axis, m):
        if m == 0:
            return value
        return lax.ppermute(value, axis, [(a, a ^ m) for a in range(lax.axis_size(axis))])

    def home(pieces):
        stacked = jnp.stack([row_send(piece, rows - k) for k, piece in enumerate(pieces)])
        twice = jnp.concatenate([stacked, stacked], 0)
        return lax.dynamic_slice_in_dim(twice, (rows - row) % rows, rows, 0)

    center = (block_input - jnp.mean(block_input, -1, keepdims=True)).astype(LOW)
    owned_x = [row_send(pick(center, (row + k) % rows), k) for k in range(rows)]
    pieces = [team_send(piece, j) for j in range(team) for piece in owned_x]

    labels = jnp.pad(expert_ids.reshape(rows, 1, local), ((0, 0), (0, 15), (0, width - local)))
    carried = jnp.concatenate([grad_out.astype(LOW), labels.astype(LOW)], 1)
    carried, pieces = lax.optimization_barrier((carried, pieces))
    owned_g = jnp.stack([row_send(pick(carried, (row + k) % rows), k) for k in range(rows)])
    grad_low = owned_g[:, :local]
    chosen = owned_g[:, local, :local].astype(jnp.int32)

    segments = lax.dynamic_slice_in_dim(segment_ids, row, 1, 0)[0]
    lows = jnp.sum((segments[:, None] < segments[None, :]).astype(jnp.int32), 0)[None, :]

    weights, out_weights = w_qkv, w_attn_out
    if padded != width:
        extra = padded - width
        weights = jnp.pad(w_qkv.reshape(width, 3, width), ((0, 0), (0, 0), (0, extra)))
        weights = weights.reshape(width, 3 * padded)
        out_weights = jnp.pad(w_attn_out, ((0, extra), (0, 0)))

    own = jnp.stack([row, member]).astype(jnp.int32)
    results = attend(own, pieces, ln1_gain, ln1_bias, weights, lows, team, rows, pairs)
    full, q, k, v, ot, logs = results[:6]
    branch = 0.0
    for j, part in enumerate(results[6:]):
        first = (member + team - j) % team * share
        weight = lax.dynamic_slice_in_dim(out_weights, first, share, 0)
        branch = branch + dot(team_send(part, j).reshape(owned, share), weight)

    residual = jnp.concatenate(owned_x, 0).astype(FULL)
    middle = residual + branch
    unit_two, inverse_two = standard(middle)
    normed_two = (unit_two * ln2_gain + ln2_bias).astype(LOW)

    relative = chosen ^ mine
    onehot = (relative[..., None] == jnp.arange(experts, dtype=jnp.int32)).astype(jnp.int32)
    rank = jnp.cumsum(onehot, 1) - onehot
    target = relative * MOST + jnp.sum(rank * onehot, -1)
    route = (
        (target[:, None, :] == jnp.arange(experts * MOST, dtype=jnp.int32)[None, :, None])
        .astype(LOW)
        .reshape(rows, experts, MOST, local)
    )
    named = (chosen[..., None] == jnp.arange(experts, dtype=jnp.int32)).astype(FULL)
    counts = jnp.sum(named, (0, 1))

    def dispatch(value):
        placed = jnp.einsum(
            "remt,rtd->ermd", route, value.reshape(rows, local, width), preferred_element_type=FULL
        )
        placed = placed.astype(LOW).reshape(experts, slots, width)
        return [swap(placed[m], "ex", m) for m in range(experts)]

    def collect(parts):
        returned = jnp.stack([swap(part, "ex", m) for m, part in enumerate(parts)])
        return jnp.einsum(
            "remt,ermd->rtd",
            route,
            returned.reshape(experts, rows, MOST, width),
            preferred_element_type=FULL,
        ).reshape(owned, width)

    grad_arrived = dispatch(grad_low)
    arrived = dispatch(normed_two)

    def shared_sum(value, rows_first):
        along_team = lambda v: team_send(v, 1)
        along_rows = lambda v: row_send(v, 1)
        cut = value.shape[0] // (team * rows)
        if rows_first:
            value = value.reshape((rows, team, cut) + value.shape[1:])
            value = ring_scatter(value, rows, row, along_rows)
            value = ring_scatter(value, team, member, along_team)
            value = ring_gather(value, team, member, along_team)
            value = ring_gather(value, rows, row, along_rows)
        else:
            value = value.reshape((team, rows, cut) + value.shape[1:])
            value = ring_scatter(value, team, member, along_team)
            value = ring_scatter(value, rows, row, along_rows)
            value = ring_gather(value, rows, row, along_rows)
            value = ring_gather(value, team, member, along_team)
        return value.reshape((-1,) + value.shape[3:]).astype(FULL)

    up_low, down_low, sums = expert(arrived, grad_arrived, w_in[0], w_down[0], 0, 2, ())
    up_high, down_high, sums = expert(arrived, grad_arrived, w_in[0], w_down[0], 1, 2, sums)
    produced, grad_rows = sums[:experts], sums[experts:]
    grad_up = jnp.concatenate([shared_sum(up_low, False), shared_sum(up_high, False)], 1)
    grad_down = jnp.concatenate([shared_sum(down_low, False), shared_sum(down_high, True)], 0)

    back_two, grad_gain_two, grad_bias_two = standard_back(
        collect(grad_rows), ln2_gain, unit_two, inverse_two
    )
    grad_branch = (back_two + grad_low.reshape(owned, width).astype(FULL)).astype(LOW)
    grad_branch = grad_branch.reshape(rows, local, width)
    grad_weights, grad_full = attend_back(
        own, [team_send(grad_branch, j) for j in range(team)], full, weights, out_weights, lows,
        q, k, v, ot, logs, team, rows, pairs,
    )

    change = (branch + collect(produced)).astype(LOW).reshape(rows, local, width)
    block_output = block_input + home(list(change)).astype(FULL)

    unit_one, inverse_one = standard(residual)
    grad_normed_one = sum(
        team_send(part, j).astype(FULL) for j, part in enumerate(grad_full)
    ).reshape(owned, width)
    back_one, grad_gain_one, grad_bias_one = standard_back(
        grad_normed_one, ln1_gain, unit_one, inverse_one
    )
    grad_change = (back_two + back_one).astype(LOW).reshape(rows, local, width)
    grad_input = grad_out + home(list(grad_change)).astype(FULL)

    cut = width // (experts * rows)
    bits = [1 << b for b in range(experts.bit_length() - 1)]
    value = grad_weights.reshape(4, experts, rows, cut, share).swapaxes(0, 1)
    for bit in bits:
        halves = value.reshape((value.shape[0] // 2, 2) + value.shape[1:])
        on = (mine // bit) % 2
        keep = lax.dynamic_index_in_dim(halves, on, 1, keepdims=False)
        give = lax.dynamic_index_in_dim(halves, 1 - on, 1, keepdims=False)
        value = add_low(keep, swap(give, "ex", bit))
    value = value[0].swapaxes(0, 1)
    value = sum(row_send(pick(value, (row + k) % rows), k).astype(FULL) for k in range(rows)).astype(LOW)
    out = jnp.zeros((rows,) + value.shape, LOW)
    for k in range(rows):
        out = lax.dynamic_update_index_in_dim(out, row_send(value, k), (row + rows - k) % rows, 0)
    value = ring_gather(out, team, member, lambda v: team_send(v, 1))[None]
    for bit in reversed(bits):
        on = (mine // bit) % 2
        other = swap(value, "ex", bit)
        pair = jnp.where(on == 0, jnp.stack([value, other], 1), jnp.stack([other, value], 1))
        value = pair.reshape((-1,) + pair.shape[2:])
    value = value.reshape(experts, team, rows, 4, cut, share)
    grad_qkv = jnp.transpose(value[:, :, :, :3], (0, 2, 4, 3, 1, 5)).reshape(width, 3, padded)
    grad_qkv = grad_qkv[..., :width].reshape(width, 3 * width).astype(FULL)
    grad_attn_out = jnp.transpose(value[:, :, :, 3], (1, 4, 0, 2, 3)).reshape(padded, width)
    grad_attn_out = grad_attn_out[:width].astype(FULL)

    small = jnp.stack(
        [
            grad_gain_one, grad_bias_one, grad_gain_two, grad_bias_two,
            jnp.pad(counts, (0, width - experts)),
        ]
    )
    for axis, size in (("ex", experts), ("seq", seq)):
        for b in range(size.bit_length() - 1):
            small = small + swap(small, axis, 1 << b)
    load = small[4, :experts] * (experts / (rows * length * experts))
    return (
        block_output, grad_input, grad_qkv, grad_attn_out, small[0], small[1], small[2], small[3],
        grad_up[None], grad_down[None], load,
    )


def solution(mesh):
    tokens = P("ex", "seq", None)
    expert_axis = P("ex", None, None)
    return jax.shard_map(
        per_device,
        mesh=mesh,
        in_specs=(
            tokens, P("ex", None), tokens, P(), P(), P(), P(), P(), P(),
            expert_axis, expert_axis, tokens,
        ),
        out_specs=(
            tokens, tokens, P(), P(), P(), P(), P(), P(), expert_axis, expert_axis, P(),
        ),
        check_vma=False,
    )
```

```python
import functools
import math

import jax
import jax.numpy as jnp
from jax import lax
from jax.experimental import pallas as pl
from jax.experimental.pallas import tpu as pltpu
from jax.sharding import PartitionSpec as P

HEADS = 12
HEAD = 64
MOST = 48
PAIR = 2 * HEAD
EPSILON = 1e-05
NEGATIVE = -1e30
LOW = jnp.bfloat16
FULL = jnp.float32
VMEM_LIMIT = 60 * 1024 * 1024
NN = (((1,), (0,)), ((), ()))
NT = (((1,), (1,)), ((), ()))
TN = (((0,), (0,)), ((), ()))


def dot(a, b, dims=NN):
    return lax.dot_general(a, b, dims, preferred_element_type=FULL)


def loop(first, last, unroll, body, carry):
    if unroll:
        for index in range(first, last):
            carry = body(index, carry)
        return carry
    return lax.fori_loop(first, last, body, carry)


def each(count, unroll, body):
    def step(index, carry):
        body(index)
        return carry

    loop(0, count, unroll, step, 0)


def tile_mask(shape, low_row, key_first, query_first, diagonal):
    key_pos = key_first + lax.broadcasted_iota(jnp.int32, shape, 0)
    allowed = key_pos >= low_row
    if diagonal:
        query_pos = query_first + lax.broadcasted_iota(jnp.int32, shape, 1)
        allowed = allowed & (key_pos <= query_pos)
    return allowed


def head_lanes(value, head):
    lane = lax.broadcasted_iota(jnp.int32, value.shape, 1)
    return jnp.where((lane // HEAD) == head, value, jnp.zeros_like(value))


def place_of(own_ref, j, k, team, rows, local):
    row = lax.rem(own_ref[0] + (rows - k), rows)
    member = lax.rem(own_ref[1] + (team + j) % team, team)
    return pl.ds(pl.multiple_of((row * team + member) * local, local), local)


def standard(value):
    center = value - jnp.mean(value, -1, keepdims=True)
    spread = jnp.mean(center * center, -1, keepdims=True)
    inverse = lax.rsqrt(spread + EPSILON)
    return center * inverse, inverse


def standard_back(grad, gain, unit, inverse):
    u = grad * gain
    lean = jnp.mean(u * unit, -1, keepdims=True)
    back = (u - jnp.mean(u, -1, keepdims=True) - unit * lean) * inverse
    return back, jnp.sum(grad * unit, 0), jnp.sum(grad, 0)


def attend_kernel(team, rows, local, block, unroll, own_ref, *refs):
    pieces, refs = refs[: team * rows], refs[team * rows :]
    gain_ref, bias_ref, wq_ref, wk_ref, wv_ref, low_ref = refs[:6]
    x_ref, q_ref, k_ref, v_ref, ot_ref, log_ref = refs[6:12]
    o_refs = refs[12 : 12 + team]
    vt_ref, o_ref = refs[12 + team :]
    length = x_ref.shape[0]
    count = length // block

    @pl.when(pl.program_id(0) == 0)
    def _():
        for j in range(team):
            for k in range(rows):
                unit, _ = standard(pieces[j * rows + k][...].astype(FULL))
                normed = unit * gain_ref[...] + bias_ref[...]
                x_ref[place_of(own_ref, -j, k, team, rows, local), :] = normed.astype(LOW)

    def project(index):
        span = pl.ds(index * block, block)
        x = x_ref[span, :]
        q_ref[span, :] = (dot(x, wq_ref[...]).astype(LOW) * LOW(HEAD**-0.5)).astype(LOW)
        k_ref[span, :] = dot(x, wk_ref[...]).astype(LOW)
        v = dot(x, wv_ref[...]).astype(LOW)
        v_ref[span, :] = v
        vt_ref[:, span] = v.T

    each(count, unroll, project)

    def one_block(qi):
        span = pl.ds(qi * block, block)
        low_row = low_ref[:, span]
        q = q_ref[span, :]
        masked = [head_lanes(q, head) for head in range(2)]

        def tile(kj, state, diagonal):
            keys = pl.ds(kj * block, block)
            k = k_ref[keys, :]
            allowed = tile_mask((block, block), low_row, kj * block, qi * block, diagonal)
            after = []
            for head in range(2):
                scores = jnp.where(allowed, dot(k, masked[head], NT), NEGATIVE)
                high = jnp.max(scores, 0, keepdims=True)
                if state is not None:
                    high = jnp.maximum(high, state[head][0])
                weights = jnp.exp(scores - high)
                total = jnp.sum(weights, 0, keepdims=True)
                summed = dot(vt_ref[pl.ds(head * HEAD, HEAD), keys], weights.astype(LOW))
                if state is not None:
                    fade = jnp.exp(state[head][0] - high)
                    total = total + state[head][1] * fade
                    summed = summed + state[head][2] * fade
                after.append((high, total, summed))
            return tuple(after)

        state = loop(
            0, qi, unroll, lambda kj, carry: tile(kj, carry, False), tile(qi, None, True)
        )
        done = []
        for head in range(2):
            high, total, summed = state[head]
            log_ref[0, pl.ds(head, 1), span] = high + jnp.log(total)
            done.append(summed / total)
        both = jnp.concatenate(done, 0)
        ot_ref[:, span] = both
        o_ref[span, :] = both.T.astype(LOW)

    each(count, unroll, one_block)
    for j in range(team):
        for k in range(rows):
            o_refs[j][k] = o_ref[place_of(own_ref, j, k, team, rows, local), :]


def attend_back_kernel(team, rows, local, block, unroll, experts, own_ref, *refs):
    pieces, refs = refs[:team], refs[team:]
    x_ref, wq_ref, wk_ref, wv_ref, wo_ref, low_ref = refs[:6]
    q_ref, k_ref, v_ref, ot_ref, log_ref = refs[6:11]
    gx_refs, refs = refs[11 : 11 + team], refs[11 + team :]
    gw_ref, b_ref, g_ref, kt_ref, delta_ref, dqt_ref, d_ref, sum_ref = refs
    length, width = x_ref.shape
    count = length // block
    scale = HEAD**-0.5
    pair = pl.program_id(0)

    @pl.when(pair == 0)
    def _():
        for j in range(team):
            for k in range(rows):
                b_ref[place_of(own_ref, -j, k, team, rows, local), :] = pieces[j][k]
        sum_ref[...] = jnp.zeros_like(sum_ref)

    def prepare(index):
        span = pl.ds(index * block, block)
        kt_ref[:, span] = k_ref[span, :].T
        g = dot(b_ref[span, :], wo_ref[...], NT).astype(LOW)
        g_ref[span, :] = g
        product = g.astype(FULL).T * ot_ref[:, span]
        for head in range(2):
            part = product[head * HEAD : (head + 1) * HEAD]
            delta_ref[pl.ds(head, 1), span] = jnp.sum(part, 0, keepdims=True)
        dqt_ref[:, span] = jnp.zeros((PAIR, block), FULL)

    each(count, unroll, prepare)

    def one_block(kj):
        keys = pl.ds(kj * block, block)
        k = k_ref[keys, :]
        v = v_ref[keys, :]

        def tile(qi, carry, diagonal):
            grad_k, grad_v = carry
            span = pl.ds(qi * block, block)
            q = q_ref[span, :]
            g = g_ref[span, :]
            allowed = tile_mask(
                (block, block), low_ref[:, span], kj * block, qi * block, diagonal
            )
            for head in range(2):
                qm = head_lanes(q, head)
                gm = head_lanes(g, head)
                part = pl.ds(head * HEAD, HEAD)
                probs = jnp.exp(dot(k, qm, NT) - log_ref[0, pl.ds(head, 1), span])
                probs = jnp.where(allowed, probs, 0.0)
                grad_probs = dot(v, gm, NT)
                grad_scores = (probs * (grad_probs - delta_ref[pl.ds(head, 1), span])).astype(LOW)
                grad_v = grad_v + dot(probs.astype(LOW), gm)
                grad_k = grad_k + dot(grad_scores, qm)
                dqt_ref[part, span] += dot(kt_ref[part, keys], grad_scores)
            return grad_k, grad_v

        zero = jnp.zeros((block, PAIR), FULL)
        grad_k, grad_v = loop(
            kj + 1,
            count,
            unroll,
            lambda qi, carry: tile(qi, carry, False),
            tile(kj, (zero, zero), True),
        )
        d_ref[keys, PAIR : 2 * PAIR] = grad_k.astype(LOW)
        d_ref[keys, 2 * PAIR :] = grad_v.astype(LOW)

    each(count, unroll, one_block)

    weight = jnp.concatenate([wq_ref[...], wk_ref[...], wv_ref[...]], 1)

    def spread(index):
        span = pl.ds(index * block, block)
        d_ref[span, :PAIR] = (dqt_ref[:, span] * scale).T.astype(LOW)
        sum_ref[span, :] += dot(d_ref[span, :], weight, NT)

    each(count, unroll, spread)

    grads = dot(x_ref[...], d_ref[...], TN).astype(LOW)
    out_grads = dot(ot_ref[...].astype(LOW), b_ref[...]).T.astype(LOW)
    cut = width // experts
    for e in range(experts):
        span = slice(e * cut, (e + 1) * cut)
        for which in range(3):
            gw_ref[e, which] = grads[span, which * PAIR : (which + 1) * PAIR]
        gw_ref[e, 3] = out_grads[span]

    @pl.when(pair == pl.num_programs(0) - 1)
    def _():
        for j in range(team):
            for k in range(rows):
                gx_refs[j][k] = sum_ref[place_of(own_ref, j, k, team, rows, local), :].astype(LOW)


def fixed(*shape):
    return pl.BlockSpec(shape, lambda p, own: (0,) * len(shape), pipeline_mode=pl.Buffered(1))


def attention_specs(length, width, pairs, all_pairs):
    weight = lambda which: pl.BlockSpec(
        (width, PAIR), lambda p, own: (0, which * all_pairs + own[1] * pairs + p)
    )
    columns = lambda: pl.BlockSpec((length, PAIR), lambda p, own: (0, p))
    across = pl.BlockSpec((PAIR, length), lambda p, own: (p, 0))
    logs = pl.BlockSpec((1, 2, length), lambda p, own: (p, 0, 0))
    return weight, columns, across, logs


def attend(own, pieces, gain, bias, weights, low, team, rows, pairs):
    local, width = pieces[0].shape
    length = team * rows * local
    share = pairs * PAIR
    block = math.gcd(length, 256)
    unroll = length // block <= 4
    weight, columns, across, logs = attention_specs(length, width, pairs, pairs * team)
    shape = jax.ShapeDtypeStruct
    return pl.pallas_call(
        functools.partial(attend_kernel, team, rows, local, block, unroll),
        grid_spec=pltpu.PrefetchScalarGridSpec(
            num_scalar_prefetch=1,
            grid=(pairs,),
            in_specs=[fixed(local, width)] * len(pieces)
            + [fixed(1, width)] * 2
            + [weight(0), weight(1), weight(2), fixed(1, length)],
            out_specs=[pl.BlockSpec((length, width), lambda p, own: (0, 0))]
            + [columns(), columns(), columns(), across, logs]
            + [pl.BlockSpec((rows, local, PAIR), lambda p, own: (0, 0, p))] * team,
            scratch_shapes=[pltpu.VMEM((PAIR, length), LOW), pltpu.VMEM((length, PAIR), LOW)],
        ),
        out_shape=[shape((length, width), LOW)]
        + [shape((length, share), LOW)] * 3
        + [shape((share, length), FULL), shape((pairs, 2, length), FULL)]
        + [shape((rows, local, share), LOW)] * team,
        compiler_params=pltpu.CompilerParams(vmem_limit_bytes=VMEM_LIMIT),
        cost_estimate=pl.CostEstimate(
            flops=2 * length * width * 3 * share + 8 * length * length * share,
            bytes_accessed=4 * length * width + 12 * length * share,
            transcendentals=length * length * pairs,
        ),
        name="attend",
    )(own, *pieces, gain[None], bias[None], weights, weights, weights, low)


def attend_back(
    own, pieces, x, weights, out_weights, low, q, k, v, ot, logs_in, team, rows, pairs, experts
):
    length, width = x.shape
    local = length // (team * rows)
    share = pairs * PAIR
    block = math.gcd(length, 256)
    unroll = length // block <= 4
    weight, columns, across, logs = attention_specs(length, width, pairs, pairs * team)
    shape = jax.ShapeDtypeStruct
    out = pl.BlockSpec((rows, local, width), lambda p, own: (0, 0, 0))
    results = pl.pallas_call(
        functools.partial(attend_back_kernel, team, rows, local, block, unroll, experts),
        grid_spec=pltpu.PrefetchScalarGridSpec(
            num_scalar_prefetch=1,
            grid=(pairs,),
            in_specs=[fixed(rows, local, width)] * team
            + [fixed(length, width), weight(0), weight(1), weight(2)]
            + [pl.BlockSpec((PAIR, width), lambda p, own: (own[1] * pairs + p, 0))]
            + [fixed(1, length), columns(), columns(), columns(), across, logs],
            out_specs=[out] * team
            + [pl.BlockSpec((experts, 4, width // experts, PAIR), lambda p, own: (0, 0, 0, p))],
            scratch_shapes=[
                pltpu.VMEM((length, width), LOW),
                pltpu.VMEM((length, PAIR), LOW),
                pltpu.VMEM((PAIR, length), LOW),
                pltpu.VMEM((2, length), FULL),
                pltpu.VMEM((PAIR, length), FULL),
                pltpu.VMEM((length, 3 * PAIR), LOW),
                pltpu.VMEM((length, width), FULL),
            ],
        ),
        out_shape=[shape((rows, local, width), LOW)] * team
        + [shape((experts, 4, width // experts, share), LOW)],
        compiler_params=pltpu.CompilerParams(vmem_limit_bytes=VMEM_LIMIT),
        cost_estimate=pl.CostEstimate(
            flops=4 * length * width * 4 * share + 20 * length * length * share,
            bytes_accessed=6 * length * width + 24 * length * share,
            transcendentals=length * length * pairs,
        ),
        name="attend_back",
    )(own, *pieces, x, weights, weights, weights, out_weights, low, q, k, v, ot, logs_in)
    return results[team], results[:team]


GELU_SCALE = math.sqrt(2.0 / math.pi)
GELU_CUBE = 0.044715


def expert_kernel(count, first, last, own_ref, *refs):
    x_refs, refs = refs[:count], refs[count:]
    g_refs, refs = refs[:count], refs[count:]
    up_ref, down_ref, refs = refs[0], refs[1], refs[2:]
    if not first:
        y_in, gx_in, refs = refs[0], refs[1], refs[2:]
    gup_ref, gdown_ref, refs = refs[0], refs[1], refs[2:]
    if last:
        y_out, gx_out, y_sum, gx_sum, refs = refs[0], refs[1], refs[2], refs[3], refs[4:]
    else:
        y_sum, gx_sum, refs = refs[0], refs[1], refs[2:]
    x_ref, g_ref = refs
    step = pl.program_id(0)
    size = x_refs[0].shape[0]

    @pl.when(step == 0)
    def _():
        for index in range(count):
            span = pl.ds(index * size, size)
            x_ref[span, :] = x_refs[index][...]
            g_ref[span, :] = g_refs[index][...]
        if first:
            y_sum[...] = jnp.zeros_like(y_sum)
            gx_sum[...] = jnp.zeros_like(gx_sum)
        else:
            y_sum[...] = y_in[...]
            gx_sum[...] = gx_in[...]

    x = x_ref[...]
    g = g_ref[...]
    inner = dot(x, up_ref[...])
    square = inner * inner
    curve = jnp.tanh(GELU_SCALE * inner * (1.0 + GELU_CUBE * square))
    half = 0.5 + 0.5 * curve
    active = (inner * half).astype(LOW)
    slope = half + (0.5 * GELU_SCALE) * inner * (1.0 - curve * curve) * (
        1.0 + (3.0 * GELU_CUBE) * square
    )
    grad_inner = (dot(g, down_ref[...], NT) * slope).astype(LOW)
    gdown_ref[...] = dot(active, g, TN).astype(LOW)
    gup_ref[...] = dot(x, grad_inner, TN).astype(LOW)
    y_sum[...] += dot(active, down_ref[...])
    gx_sum[...] += dot(grad_inner, up_ref[...], NT)

    if last:

        @pl.when(step == pl.num_programs(0) - 1)
        def _():
            for index in range(count):
                span = pl.ds(index * size, size)
                y_out[own_ref[2] ^ index] = y_sum[span, :].astype(LOW)
                gx_out[own_ref[2] ^ index] = gx_sum[span, :].astype(LOW)


def expert(own, xs, gs, up, down, part, parts, sums):
    count = len(xs)
    size, width = xs[0].shape
    hidden = up.shape[1] // parts
    block = math.gcd(hidden, 512)
    steps = hidden // block
    first, last = part == 0, part == parts - 1
    rows = pl.BlockSpec((size, width), lambda f, own: (0, 0))
    whole = pl.BlockSpec((count * size, width), lambda f, own: (0, 0))
    every = pl.BlockSpec((count, size, width), lambda f, own: (0, 0, 0))
    shape = jax.ShapeDtypeStruct
    sum_shape = shape((count * size, width), FULL)
    in_specs = [rows] * (2 * count) + [
        pl.BlockSpec((width, block), lambda f, own: (0, f + part * steps)),
        pl.BlockSpec((block, width), lambda f, own: (f + part * steps, 0)),
    ]
    out_specs = [
        pl.BlockSpec((width, block), lambda f, own: (0, f)),
        pl.BlockSpec((block, width), lambda f, own: (f, 0)),
    ]
    out_shape = [shape((width, hidden), LOW), shape((hidden, width), LOW)]
    scratch = []
    if not first:
        in_specs += [whole] * 2
    if last:
        out_specs += [every] * 2
        out_shape += [shape((count, size, width), LOW)] * 2
        scratch += [pltpu.VMEM(sum_shape.shape, FULL)] * 2
    else:
        out_specs += [whole] * 2
        out_shape += [sum_shape] * 2
    results = pl.pallas_call(
        functools.partial(expert_kernel, count, first, last),
        grid_spec=pltpu.PrefetchScalarGridSpec(
            num_scalar_prefetch=1,
            grid=(steps,),
            in_specs=in_specs,
            out_specs=out_specs,
            scratch_shapes=scratch + [pltpu.VMEM((count * size, width), LOW)] * 2,
        ),
        out_shape=out_shape,
        compiler_params=pltpu.CompilerParams(vmem_limit_bytes=VMEM_LIMIT),
        cost_estimate=pl.CostEstimate(
            flops=12 * count * size * width * hidden,
            bytes_accessed=8 * width * hidden + 8 * count * size * width,
            transcendentals=count * size * hidden,
        ),
        name="expert",
    )(own, *xs, *gs, up, down, *sums)
    return results[0], results[1], results[2:]


def tie(values, others):
    count, total = len(values), len(values) + len(others)
    return pl.pallas_call(
        lambda *refs: None,
        in_specs=[pl.BlockSpec(memory_space=pl.ANY)] * total,
        out_specs=[pl.BlockSpec(memory_space=pl.ANY)] * count,
        out_shape=[jax.ShapeDtypeStruct(value.shape, value.dtype) for value in values],
        input_output_aliases={index: index for index in range(count)},
        name="tie",
    )(*values, *others)


def put_kernel(count, joined, place, own_ref, *refs):
    out_ref = refs[count + joined]
    size, cut, _ = refs[0].shape
    for i in range(count):
        for n in range(size):
            first = pl.multiple_of(place(own_ref, i, n) * cut, cut)
            out_ref[pl.ds(first, cut), :] = refs[i][n].astype(FULL)


def put_chunk(own, parts, into, shape, block, place):
    count, (size, cut, width) = len(parts), parts[0].shape
    joined = [] if into is None else [into]
    return pl.pallas_call(
        functools.partial(put_kernel, count, len(joined), place),
        grid_spec=pltpu.PrefetchScalarGridSpec(
            num_scalar_prefetch=1,
            grid=(1,),
            in_specs=[pl.BlockSpec((size, cut, width), lambda s, own: (0, 0, 0))] * count
            + [pl.BlockSpec(memory_space=pl.ANY)] * len(joined),
            out_specs=pl.BlockSpec((count * size * cut, width), lambda s, own: block),
        ),
        out_shape=jax.ShapeDtypeStruct(shape, FULL),
        input_output_aliases={1 + count: 0} if joined else {},
        compiler_params=pltpu.CompilerParams(vmem_limit_bytes=VMEM_LIMIT),
        cost_estimate=pl.CostEstimate(
            flops=0, bytes_accessed=8 * count * size * cut * width, transcendentals=0
        ),
        name="put_chunk",
    )(own, *parts, *joined)


def place_kernel(team, rows, experts, own_ref, *refs):
    parts, (qkv_ref, out_ref, hold_ref) = refs[: team * experts], refs[team * experts :]
    cut, share = parts[0].shape[2:]
    which = pl.program_id(0)

    def rows_of(m, k):
        index = (own_ref[2] ^ m) * rows + k
        return pl.ds(pl.multiple_of(index * cut, cut), cut)

    for j in range(team):
        member = lax.rem(own_ref[1] + (team - j), team)
        span = pl.ds(pl.multiple_of(member * share, share), share)

        @pl.when(which < 3)
        def _():
            for m in range(experts):
                for k in range(rows):
                    part = parts[m * team + j][k, 0]
                    qkv_ref[rows_of(m, k), span] = part.astype(FULL)

        @pl.when(which == 3)
        def _():
            for m in range(experts):
                for k in range(rows):
                    part = parts[m * team + j][k, 0]
                    hold_ref[rows_of(m, k), :] = part.astype(FULL)
            out_ref[span, :] = hold_ref[...].T


def place_weights(own, parts, team, rows, experts):
    _, _, cut, share = parts[0].shape
    width, padded = experts * rows * cut, team * share
    return pl.pallas_call(
        functools.partial(place_kernel, team, rows, experts),
        grid_spec=pltpu.PrefetchScalarGridSpec(
            num_scalar_prefetch=1,
            grid=(4,),
            in_specs=[pl.BlockSpec((rows, 1, cut, share), lambda w, own: (0, w, 0, 0))]
            * (team * experts),
            out_specs=[
                pl.BlockSpec((width, padded), lambda w, own: (0, jnp.minimum(w, 2))),
                pl.BlockSpec((padded, width), lambda w, own: (0, 0)),
            ],
            scratch_shapes=[pltpu.VMEM((width, share), FULL)],
        ),
        out_shape=[
            jax.ShapeDtypeStruct((width, 3 * padded), FULL),
            jax.ShapeDtypeStruct((padded, width), FULL),
        ],
        compiler_params=pltpu.CompilerParams(vmem_limit_bytes=VMEM_LIMIT),
        cost_estimate=pl.CostEstimate(
            flops=0, bytes_accessed=24 * width * padded, transcendentals=0
        ),
        name="place_weights",
    )(own, *parts)


def norm_back_kernel(team, own_ref, *refs):
    parts, refs = refs[:team], refs[team:]
    x_ref, more_ref, gain_ref, out_ref, sum_ref = refs
    unit, inverse = standard(x_ref[0].astype(FULL))
    grad = parts[0][0].astype(FULL)
    for part in parts[1:]:
        grad = grad + part[0].astype(FULL)
    back, gain, bias = standard_back(grad, gain_ref[...], unit, inverse)
    out_ref[0] = (back + more_ref[0].astype(FULL)).astype(LOW)

    @pl.when(pl.program_id(0) == 0)
    def _():
        sum_ref[...] = jnp.zeros_like(sum_ref)

    sum_ref[0:1, :] += gain[None]
    sum_ref[1:2, :] += bias[None]


def norm_back(own, parts, x, more, gain):
    rows, local, width = x.shape
    block = pl.BlockSpec((1, local, width), lambda k, own: (k, 0, 0))
    home = lambda k, own: (lax.rem(own[0] + (rows - k), rows), 0, 0)
    return pl.pallas_call(
        functools.partial(norm_back_kernel, len(parts)),
        grid_spec=pltpu.PrefetchScalarGridSpec(
            num_scalar_prefetch=1,
            grid=(rows,),
            in_specs=[block] * (len(parts) + 2)
            + [pl.BlockSpec((1, width), lambda k, own: (0, 0))],
            out_specs=[
                pl.BlockSpec((1, local, width), home),
                pl.BlockSpec((8, width), lambda k, own: (0, 0)),
            ],
        ),
        out_shape=[
            jax.ShapeDtypeStruct(x.shape, LOW),
            jax.ShapeDtypeStruct((8, width), FULL),
        ],
        cost_estimate=pl.CostEstimate(flops=0, bytes_accessed=40 * x.size, transcendentals=0),
        name="norm_back",
    )(own, *parts, x, more, gain[None])


def add_low(a, b):
    return (a.astype(FULL) + b.astype(FULL)).astype(LOW)


def pick(value, index):
    return lax.dynamic_index_in_dim(value, index, 0, keepdims=False)


def ring_scatter(value, size, place, send):
    total = pick(value, (place + size - 1) % size)
    for step in range(size - 1):
        total = add_low(send(total), pick(value, (place + 2 * size - 2 - step) % size))
    return total


def ring_gather(value, size, place, send):
    out = jnp.zeros((size,) + value.shape, value.dtype)
    out = lax.dynamic_update_index_in_dim(out, value, place, 0)
    for step in range(size - 1):
        value = send(value)
        out = lax.dynamic_update_index_in_dim(out, value, (place + size - 1 - step) % size, 0)
    return out


def per_device(
    block_input, segment_ids, expert_ids, ln1_gain, ln1_bias, ln2_gain, ln2_bias,
    w_qkv, w_attn_out, w_in, w_down, grad_out,
):
    rows, local, width = block_input.shape
    seq = lax.axis_size("seq")
    experts = lax.axis_size("ex")
    team = seq // rows
    length = seq * local
    owned = rows * local
    pairs = -(-HEADS // (2 * team))
    share = pairs * PAIR
    padded = share * team
    place = lax.axis_index("seq")
    mine = lax.axis_index("ex")
    row, member = place // team, place % team
    slots = rows * MOST

    def row_send(value, k):
        if k % rows == 0:
            return value
        pattern = [(a * team + b, (a + k) % rows * team + b) for a in range(rows) for b in range(team)]
        return lax.ppermute(value, "seq", pattern)

    def team_send(value, j):
        if j % team == 0:
            return value
        pattern = [(a * team + b, a * team + (b + j) % team) for a in range(rows) for b in range(team)]
        return lax.ppermute(value, "seq", pattern)

    def swap(value, axis, m):
        if m == 0 or m >= lax.axis_size(axis):
            return value
        return lax.ppermute(value, axis, [(a, a ^ m) for a in range(lax.axis_size(axis))])

    across_rows = [[r * team + g for r in range(rows)] for g in range(team)]

    def swap_rows(value):
        return lax.all_to_all(value, "seq", 0, 0, tiled=True, axis_index_groups=across_rows)

    def swap_experts(value):
        return lax.all_to_all(value, "ex", 0, 0, tiled=True)

    center = (block_input - jnp.mean(block_input, -1, keepdims=True)).astype(LOW)
    owned_x = [row_send(pick(center, (row + k) % rows), k) for k in range(rows)]
    pieces = [team_send(piece, j) for j in range(team) for piece in owned_x]

    labels = jnp.pad(expert_ids.reshape(rows, 1, local), ((0, 0), (0, 15), (0, width - local)))
    carried = jnp.concatenate([grad_out.astype(LOW), labels.astype(LOW)], 1)
    carried = tie([carried], [owned_x[1]])[0]
    owned_g = jnp.stack([row_send(pick(carried, (row + k) % rows), k) for k in range(rows)])
    grad_low = owned_g[:, :local]
    chosen = owned_g[:, local, :local].astype(jnp.int32)

    segments = lax.dynamic_slice_in_dim(segment_ids, row, 1, 0)[0]
    lows = jnp.sum((segments[:, None] < segments[None, :]).astype(jnp.int32), 0)[None, :]

    weights, out_weights = w_qkv, w_attn_out
    if padded != width:
        extra = padded - width
        weights = jnp.pad(w_qkv.reshape(width, 3, width), ((0, 0), (0, 0), (0, extra)))
        weights = weights.reshape(width, 3 * padded)
        out_weights = jnp.pad(w_attn_out, ((0, extra), (0, 0)))

    own = jnp.stack([row, member, mine]).astype(jnp.int32)
    results = attend(own, pieces, ln1_gain, ln1_bias, weights, lows, team, rows, pairs)
    full, q, k, v, ot, logs = results[:6]
    branch = 0.0
    for j, part in enumerate(tie(results[6:], [owned_g])):
        first = (member + team - j) % team * share
        weight = lax.dynamic_slice_in_dim(out_weights, first, share, 0)
        branch = branch + dot(team_send(part, j).reshape(owned, share), weight)

    residual = jnp.concatenate(owned_x, 0).astype(FULL)
    middle = residual + branch
    unit_two, inverse_two = standard(middle)
    normed_two = (unit_two * ln2_gain + ln2_bias).astype(LOW)

    relative = chosen ^ mine
    onehot = (relative[..., None] == jnp.arange(experts, dtype=jnp.int32)).astype(jnp.int32)
    rank = jnp.cumsum(onehot, 1) - onehot
    target = relative * MOST + jnp.sum(rank * onehot, -1)
    numbers = jnp.arange(experts * MOST, dtype=jnp.int32)[None, :, None]

    def routes(target):
        match = (target[:, None, :] == numbers).astype(LOW)
        return match.reshape(rows, experts, MOST, local)

    route = routes(target)
    back_route = routes((target // MOST ^ mine) * MOST + target % MOST)
    named = (chosen[..., None] == jnp.arange(experts, dtype=jnp.int32)).astype(FULL)
    counts = jnp.sum(named, (0, 1))

    def dispatch(value):
        placed = jnp.einsum(
            "remt,rtd->ermd", route, value.reshape(rows, local, width), preferred_element_type=FULL
        )
        placed = placed.astype(LOW).reshape(experts, slots, width)
        return [swap(placed[m], "ex", m) for m in range(experts)]

    def collect(returned):
        return jnp.einsum(
            "remt,ermd->rtd",
            back_route,
            returned.reshape(experts, rows, MOST, width),
            preferred_element_type=FULL,
        ).reshape(owned, width)

    grad_arrived = dispatch(grad_low)
    arrived = dispatch(normed_two)

    hops = rows - 1

    def along_team(value):
        return team_send(value, 1)

    def team_scatter(value):
        return ring_scatter(value, team, member, along_team)

    def team_gather(value):
        return [team_send(value, j) for j in range(team)]

    def cut_up(value, sizes):
        return value.reshape(sizes + (value.shape[0] // seq,) + value.shape[1:])

    def first_hop(value):
        return row_send(pick(value, (row + rows - 1) % rows), 1)

    def joined(came, value, step):
        return add_low(came, pick(value, (row + 2 * rows - 2 - step) % rows))

    def next_hop(came, value, step):
        return row_send(joined(came, value, step), 1)

    def sync(*values):
        leaves, tree = jax.tree.flatten(values)
        return jax.tree.unflatten(tree, tie(leaves, []))

    def team_first(own_ref, i, n):
        device = lax.rem(own_ref[1] + (team - i), team)
        return device * rows + lax.rem(own_ref[0] + (rows - n), rows)

    def rows_first(own_ref, i, n):
        device = lax.rem(own_ref[1] + (team - n), team)
        return lax.rem(own_ref[0] + (rows - i), rows) * team + device

    up_shape, down_shape = w_in.shape[1:], w_down.shape[1:]

    up_one, down_one, sums = expert(own, arrived, grad_arrived, w_in[0], w_down[0], 0, 2, ())
    cut_a = cut_up(up_one, (team, rows))
    middle_row = cut_a.shape[2] // 2
    cut_z = cut_up(down_one, (rows, team))
    first_a = team_scatter(cut_a[:, :, :middle_row])
    z = first_hop(cut_z)
    up_two, down_two, sums = expert(own, arrived, grad_arrived, w_in[0], w_down[0], 1, 2, sums)
    produced, grad_rows = sums
    rest_a = cut_a[:, :, middle_row:]
    z, produced, grad_rows, rest_a = sync(z, produced, grad_rows, rest_a)

    grad_rows = swap_experts(grad_rows)
    z = next_hop(z, cut_z, 0)
    rest_a = team_scatter(rest_a)
    grad_rows, produced, first_a = sync(grad_rows, produced, first_a)

    produced = swap_experts(produced)
    back_two, grad_gain_two, grad_bias_two = standard_back(
        collect(grad_rows), ln2_gain, unit_two, inverse_two
    )
    grad_branch = (back_two + grad_low.reshape(owned, width).astype(FULL)).astype(LOW)
    grad_branch = grad_branch.reshape(rows, local, width)
    grad_branch, z = sync(grad_branch, z)

    branches = [team_send(grad_branch, j) for j in range(team)]
    z = next_hop(z, cut_z, 1)
    half_a = jnp.concatenate([first_a, rest_a], 1)
    half_a, up_two, down_two = sync(half_a, up_two, down_two)

    a = first_hop(half_a)
    half_b = team_scatter(cut_up(up_two, (team, rows)))
    z, produced = sync(z, produced)

    z = joined(z, cut_z, 2)
    change = (branch + collect(produced)).astype(LOW).reshape(rows, local, width)
    change = jnp.stack([change[(rows - n) % rows] for n in range(rows)] * 2)
    change = lax.dynamic_slice_in_dim(change, (rows - row) % rows, rows, 0)
    a, change = sync(a, change)

    a = next_hop(a, half_a, 0)
    a, branches, down_two, change = sync(a, branches, down_two, change)

    a = next_hop(a, half_a, 1)
    change = swap_rows(change)
    half_c = team_scatter(cut_up(down_two, (team, rows)))
    grads, grad_full = attend_back(
        own, branches, full, weights, out_weights, lows, q, k, v, ot, logs,
        team, rows, pairs, experts,
    )
    half_b, a, z, grads, grad_full = sync(half_b, a, z, grads, grad_full)

    grads = swap_experts(grads)
    grad_full = [team_send(part, j) for j, part in enumerate(grad_full)]
    b = first_hop(half_b)
    a = joined(a, half_a, 2)
    change, half_c, a, z = sync(change, half_c, a, z)

    pieces_a = [a, row_send(a, 1)]
    z = team_scatter(z)
    block_output = block_input + change.astype(FULL)
    b, block_output = sync(b, block_output)

    b = next_hop(b, half_b, 0)
    pieces_a = sync(pieces_a)[0]

    pieces_a = pieces_a + [row_send(pieces_a[-1], 1)]
    b, grads = sync(b, grads)

    b = next_hop(b, half_b, 1)
    cut = width // (experts * rows)
    grads = jnp.sum(grads.astype(FULL), 0).astype(LOW).reshape(4, rows, cut, share)
    grads = swap_rows(grads.swapaxes(0, 1))
    pieces_a, grad_full = sync(pieces_a, grad_full)

    pieces_a = pieces_a + [row_send(pieces_a[-1], 1)]
    grad_change, norm_sums = norm_back(
        own, grad_full, jnp.stack(owned_x), back_two.reshape(rows, local, width), ln1_gain
    )
    b, z, grad_change, norm_sums = sync(b, z, grad_change, norm_sums)

    b = joined(b, half_b, 2)
    pieces_b = [b, row_send(b, 1)]
    z = jnp.stack(team_gather(z))
    small = jnp.stack(
        [
            norm_sums[0], norm_sums[1], grad_gain_two, grad_bias_two,
            jnp.pad(counts, (0, width - experts)),
        ]
    )
    small = small + swap(small, "ex", 1)
    pieces_a, half_c = sync(pieces_a, half_c)

    c = first_hop(half_c)
    all_a = team_gather(jnp.stack(pieces_a))
    pieces_b, grads = sync(pieces_b, grads)

    pieces_b = pieces_b + [row_send(pieces_b[-1], 1)]
    grads = jnp.sum(grads.astype(FULL), 0).astype(LOW)
    grads = swap_rows(jnp.broadcast_to(grads[None], (rows,) + grads.shape))
    c, small = sync(c, small)

    c = next_hop(c, half_c, 0)
    small = small + swap(small, "ex", 2)
    pieces_b = sync(pieces_b)[0]

    pieces_b = pieces_b + [row_send(pieces_b[-1], 1)]
    c, z = sync(c, z)

    c = next_hop(c, half_c, 1)
    pieces_b, grads, all_a = sync(pieces_b, grads, all_a)

    share_grads = team_gather(grads)
    all_b = team_gather(jnp.stack(pieces_b))
    pieces_z = [z, row_send(z, 1)]
    grad_up = put_chunk(own, all_a, None, up_shape, (0, 0), team_first)
    c, small, grad_up = sync(c, small, grad_up)

    c = joined(c, half_c, 2)
    pieces_c = [c, row_send(c, 1)]
    small = small + swap(small, "seq", 1)
    pieces_z = sync(pieces_z)[0]

    pieces_z = pieces_z + [row_send(pieces_z[-1], 1)]
    pieces_c, share_grads = sync(pieces_c, share_grads)

    pieces_c = pieces_c + [row_send(pieces_c[-1], 1)]
    far_grads = [swap(part, "ex", 2) for part in share_grads]
    pieces_z, small, grad_change = sync(pieces_z, small, grad_change)

    pieces_z = pieces_z + [row_send(pieces_z[-1], 1)]
    small = small + swap(small, "seq", 2)
    pieces_c, all_b, far_grads, share_grads = sync(pieces_c, all_b, far_grads, share_grads)

    pieces_c = pieces_c + [row_send(pieces_c[-1], 1)]
    near = [swap(part, "ex", 1) for part in share_grads]
    far = [swap(part, "ex", 1) for part in far_grads]
    grad_up = put_chunk(own, all_b, grad_up, up_shape, (0, 1), team_first)
    pieces_z, small, grad_up = sync(pieces_z, small, grad_up)

    grad_change = swap_rows(grad_change)
    for bit in range(2, seq.bit_length() - 1):
        small = small + swap(small, "seq", 1 << bit)
    pieces_c, near, far, share_grads, far_grads = sync(
        pieces_c, near, far, share_grads, far_grads
    )

    all_c = team_gather(jnp.stack(pieces_c))
    parts = share_grads + near + far_grads + far
    grad_qkv, grad_attn_out = place_weights(own, parts, team, rows, experts)
    grad_down = put_chunk(own, pieces_z, None, down_shape, (0, 0), rows_first)
    grad_input = grad_out + grad_change.astype(FULL)
    all_c, grad_qkv, grad_input, grad_down = sync(all_c, grad_qkv, grad_input, grad_down)

    if padded != width:
        grad_qkv = grad_qkv.reshape(width, 3, padded)[..., :width].reshape(width, 3 * width)
        grad_attn_out = grad_attn_out[:width]
    grad_down = put_chunk(own, all_c, grad_down, down_shape, (1, 0), team_first)
    load = small[4, :experts] * (experts / (rows * length * experts))
    return (
        block_output, grad_input, grad_qkv, grad_attn_out, small[0], small[1], small[2],
        small[3], grad_up[None], grad_down[None], load,
    )


def solution(mesh):
    tokens = P("ex", "seq", None)
    expert_axis = P("ex", None, None)
    return jax.shard_map(
        per_device,
        mesh=mesh,
        in_specs=(
            tokens, P("ex", None), tokens, P(), P(), P(), P(), P(), P(),
            expert_axis, expert_axis, tokens,
        ),
        out_specs=(
            tokens, tokens, P(), P(), P(), P(), P(), P(), expert_axis, expert_axis, P(),
        ),
        check_vma=False,
    )
```

```python
import functools
import math

import jax
import jax.numpy as jnp
from jax import lax
from jax.experimental import pallas as pl
from jax.experimental.pallas import tpu as pltpu
from jax.sharding import PartitionSpec as P

HEADS = 12
HEAD = 64
MOST = 48
PAIR = 2 * HEAD
EPSILON = 1e-05
NEGATIVE = -1e30
LOW = jnp.bfloat16
FULL = jnp.float32
VMEM_LIMIT = 60 * 1024 * 1024
NN = (((1,), (0,)), ((), ()))
NT = (((1,), (1,)), ((), ()))
TN = (((0,), (0,)), ((), ()))


def dot(a, b, dims=NN):
    return lax.dot_general(a, b, dims, preferred_element_type=FULL)


def loop(first, last, unroll, body, carry):
    if unroll:
        for index in range(first, last):
            carry = body(index, carry)
        return carry
    return lax.fori_loop(first, last, body, carry)


def each(count, unroll, body):
    def step(index, carry):
        body(index)
        return carry

    loop(0, count, unroll, step, 0)


def tile_mask(shape, low_row, key_first, query_first, diagonal):
    key_pos = key_first + lax.broadcasted_iota(jnp.int32, shape, 0)
    allowed = key_pos >= low_row
    if diagonal:
        query_pos = query_first + lax.broadcasted_iota(jnp.int32, shape, 1)
        allowed = allowed & (key_pos <= query_pos)
    return allowed


def head_lanes(value, head):
    lane = lax.broadcasted_iota(jnp.int32, value.shape, 1)
    return jnp.where((lane // HEAD) == head, value, jnp.zeros_like(value))


def place_of(own_ref, j, k, team, rows, local):
    row = lax.rem(own_ref[0] + (rows - k), rows)
    member = lax.rem(own_ref[1] + (team + j) % team, team)
    return pl.ds(pl.multiple_of((row * team + member) * local, local), local)


def standard(value):
    center = value - jnp.mean(value, -1, keepdims=True)
    spread = jnp.mean(center * center, -1, keepdims=True)
    inverse = lax.rsqrt(spread + EPSILON)
    return center * inverse, inverse


def standard_back(grad, gain, unit, inverse):
    u = grad * gain
    lean = jnp.mean(u * unit, -1, keepdims=True)
    back = (u - jnp.mean(u, -1, keepdims=True) - unit * lean) * inverse
    return back, jnp.sum(grad * unit, 0), jnp.sum(grad, 0)


def attend_kernel(team, rows, local, block, unroll, own_ref, *refs):
    pieces, refs = refs[: team * rows], refs[team * rows :]
    gain_ref, bias_ref, wq_ref, wk_ref, wv_ref, low_ref = refs[:6]
    x_ref, q_ref, k_ref, v_ref, ot_ref, log_ref = refs[6:12]
    o_refs = refs[12 : 12 + team]
    vt_ref, o_ref = refs[12 + team :]
    length = x_ref.shape[0]
    count = length // block

    @pl.when(pl.program_id(0) == 0)
    def _():
        for j in range(team):
            for k in range(rows):
                unit, _ = standard(pieces[j * rows + k][...].astype(FULL))
                normed = unit * gain_ref[...] + bias_ref[...]
                x_ref[place_of(own_ref, -j, k, team, rows, local), :] = normed.astype(LOW)

    weight = jnp.concatenate([wq_ref[...], wk_ref[...], wv_ref[...]], 1)

    def project(index):
        span = pl.ds(index * block, block)
        both = dot(x_ref[span, :], weight).astype(LOW)
        q_ref[span, :] = both[:, :PAIR] * LOW(HEAD**-0.5)
        k_ref[span, :] = both[:, PAIR : 2 * PAIR]
        v = both[:, 2 * PAIR :]
        v_ref[span, :] = v
        vt_ref[:, span] = v.T

    each(count, unroll, project)

    def one_block(qi):
        span = pl.ds(qi * block, block)
        low_row = low_ref[:, span]
        q = q_ref[span, :]

        def scores_of(head, first, size, diagonal):
            scores = dot(k_ref[pl.ds(first, size), :], head_lanes(q, head), NT)
            allowed = tile_mask((size, block), low_row, first, qi * block, diagonal)
            return jnp.where(allowed, scores, NEGATIVE)

        def summed_of(head, first, size, weights):
            values = vt_ref[pl.ds(head * HEAD, HEAD), pl.ds(first, size)]
            return dot(values, weights.astype(LOW))

        def at_once(head):
            spans = [(0, qi * block, False), (qi * block, block, True)]
            spans = [(first, size, last) for first, size, last in spans if size]
            tiles = [scores_of(head, *part) for part in spans]
            high = functools.reduce(
                jnp.maximum, [jnp.max(tile, 0, keepdims=True) for tile in tiles]
            )
            tiles = [jnp.exp(tile - high) for tile in tiles]
            total = sum(jnp.sum(tile, 0, keepdims=True) for tile in tiles)
            summed = sum(
                summed_of(head, first, size, tile) for (first, size, _), tile in zip(spans, tiles)
            )
            return high, total, summed

        def in_turn(head):
            def step(kj, state, diagonal):
                scores = scores_of(head, kj * block, block, diagonal)
                high = jnp.max(scores, 0, keepdims=True)
                if state is not None:
                    high = jnp.maximum(high, state[0])
                weights = jnp.exp(scores - high)
                total = jnp.sum(weights, 0, keepdims=True)
                summed = summed_of(head, kj * block, block, weights)
                if state is not None:
                    fade = jnp.exp(state[0] - high)
                    total, summed = total + state[1] * fade, summed + state[2] * fade
                return high, total, summed

            return lax.fori_loop(
                0, qi, lambda kj, state: step(kj, state, False), step(qi, None, True)
            )

        done = []
        for head in range(2):
            high, total, summed = at_once(head) if unroll else in_turn(head)
            log_ref[0, pl.ds(head, 1), span] = high + jnp.log(total)
            done.append(summed / total)
        both = jnp.concatenate(done, 0)
        ot_ref[:, span] = both
        o_ref[span, :] = both.T.astype(LOW)

    each(count, unroll, one_block)
    for j in range(team):
        for k in range(rows):
            o_refs[j][k] = o_ref[place_of(own_ref, j, k, team, rows, local), :]


def attend_back_kernel(team, rows, local, block, unroll, experts, own_ref, *refs):
    pieces, refs = refs[:team], refs[team:]
    x_ref, wq_ref, wk_ref, wv_ref, wo_ref, low_ref = refs[:6]
    q_ref, k_ref, v_ref, ot_ref, log_ref = refs[6:11]
    gx_refs, refs = refs[11 : 11 + team], refs[11 + team :]
    gw_ref, b_ref, g_ref, kt_ref, delta_ref, dqt_ref, d_ref, sum_ref = refs
    length, width = x_ref.shape
    count = length // block
    scale = HEAD**-0.5
    pair = pl.program_id(0)

    @pl.when(pair == 0)
    def _():
        for j in range(team):
            for k in range(rows):
                b_ref[place_of(own_ref, -j, k, team, rows, local), :] = pieces[j][k]
        sum_ref[...] = jnp.zeros_like(sum_ref)

    def prepare(index):
        span = pl.ds(index * block, block)
        kt_ref[:, span] = k_ref[span, :].T
        g = dot(b_ref[span, :], wo_ref[...], NT).astype(LOW)
        g_ref[span, :] = g
        product = g.astype(FULL).T * ot_ref[:, span]
        for head in range(2):
            part = product[head * HEAD : (head + 1) * HEAD]
            delta_ref[pl.ds(head, 1), span] = jnp.sum(part, 0, keepdims=True)
        dqt_ref[:, span] = jnp.zeros((PAIR, block), FULL)

    each(count, unroll, prepare)

    def one_block(kj):
        keys = pl.ds(kj * block, block)
        k = k_ref[keys, :]
        v = v_ref[keys, :]

        def tile(qi, carry, diagonal):
            grad_k, grad_v = carry
            span = pl.ds(qi * block, block)
            q = q_ref[span, :]
            g = g_ref[span, :]
            allowed = tile_mask(
                (block, block), low_ref[:, span], kj * block, qi * block, diagonal
            )
            for head in range(2):
                qm = head_lanes(q, head)
                gm = head_lanes(g, head)
                part = pl.ds(head * HEAD, HEAD)
                probs = jnp.exp(dot(k, qm, NT) - log_ref[0, pl.ds(head, 1), span])
                probs = jnp.where(allowed, probs, 0.0)
                grad_probs = dot(v, gm, NT)
                grad_scores = (probs * (grad_probs - delta_ref[pl.ds(head, 1), span])).astype(LOW)
                grad_v = grad_v + dot(probs.astype(LOW), gm)
                grad_k = grad_k + dot(grad_scores, qm)
                dqt_ref[part, span] += dot(kt_ref[part, keys], grad_scores)
            return grad_k, grad_v

        zero = jnp.zeros((block, PAIR), FULL)
        grad_k, grad_v = loop(
            kj + 1,
            count,
            unroll,
            lambda qi, carry: tile(qi, carry, False),
            tile(kj, (zero, zero), True),
        )
        d_ref[keys, PAIR : 2 * PAIR] = grad_k.astype(LOW)
        d_ref[keys, 2 * PAIR :] = grad_v.astype(LOW)

    each(count, unroll, one_block)

    weight = jnp.concatenate([wq_ref[...], wk_ref[...], wv_ref[...]], 1)

    def spread(index):
        span = pl.ds(index * block, block)
        d_ref[span, :PAIR] = (dqt_ref[:, span] * scale).T.astype(LOW)
        sum_ref[span, :] += dot(d_ref[span, :], weight, NT)

    each(count, unroll, spread)

    grads = dot(x_ref[...], d_ref[...], TN).astype(LOW)
    out_grads = dot(ot_ref[...].astype(LOW), b_ref[...]).T.astype(LOW)
    cut = width // experts
    for e in range(experts):
        span = slice(e * cut, (e + 1) * cut)
        for which in range(3):
            gw_ref[e, which] = grads[span, which * PAIR : (which + 1) * PAIR]
        gw_ref[e, 3] = out_grads[span]

    @pl.when(pair == pl.num_programs(0) - 1)
    def _():
        for j in range(team):
            for k in range(rows):
                gx_refs[j][k] = sum_ref[place_of(own_ref, j, k, team, rows, local), :].astype(LOW)


def fixed(*shape):
    return pl.BlockSpec(shape, lambda p, own: (0,) * len(shape), pipeline_mode=pl.Buffered(1))


def attention_specs(length, width, pairs, all_pairs):
    weight = lambda which: pl.BlockSpec(
        (width, PAIR), lambda p, own: (0, which * all_pairs + own[1] * pairs + p)
    )
    columns = lambda: pl.BlockSpec((length, PAIR), lambda p, own: (0, p))
    across = pl.BlockSpec((PAIR, length), lambda p, own: (p, 0))
    logs = pl.BlockSpec((1, 2, length), lambda p, own: (p, 0, 0))
    return weight, columns, across, logs


def attend(own, pieces, gain, bias, weights, low, team, rows, pairs):
    local, width = pieces[0].shape
    length = team * rows * local
    share = pairs * PAIR
    block = math.gcd(length, 512)
    unroll = length // block <= 4
    weight, columns, across, logs = attention_specs(length, width, pairs, pairs * team)
    shape = jax.ShapeDtypeStruct
    return pl.pallas_call(
        functools.partial(attend_kernel, team, rows, local, block, unroll),
        grid_spec=pltpu.PrefetchScalarGridSpec(
            num_scalar_prefetch=1,
            grid=(pairs,),
            in_specs=[fixed(local, width)] * len(pieces)
            + [fixed(1, width)] * 2
            + [weight(0), weight(1), weight(2), fixed(1, length)],
            out_specs=[pl.BlockSpec((length, width), lambda p, own: (0, 0))]
            + [columns(), columns(), columns(), across, logs]
            + [pl.BlockSpec((rows, local, PAIR), lambda p, own: (0, 0, p))] * team,
            scratch_shapes=[pltpu.VMEM((PAIR, length), LOW), pltpu.VMEM((length, PAIR), LOW)],
        ),
        out_shape=[shape((length, width), LOW)]
        + [shape((length, share), LOW)] * 3
        + [shape((share, length), FULL), shape((pairs, 2, length), FULL)]
        + [shape((rows, local, share), LOW)] * team,
        compiler_params=pltpu.CompilerParams(vmem_limit_bytes=VMEM_LIMIT),
        cost_estimate=pl.CostEstimate(
            flops=2 * length * width * 3 * share + 8 * length * length * share,
            bytes_accessed=4 * length * width + 12 * length * share,
            transcendentals=length * length * pairs,
        ),
        name="attend",
    )(own, *pieces, gain[None], bias[None], weights, weights, weights, low)


def attend_back(
    own, pieces, x, weights, out_weights, low, q, k, v, ot, logs_in, team, rows, pairs, experts
):
    length, width = x.shape
    local = length // (team * rows)
    share = pairs * PAIR
    block = math.gcd(length, 512)
    unroll = length // block <= 4
    weight, columns, across, logs = attention_specs(length, width, pairs, pairs * team)
    shape = jax.ShapeDtypeStruct
    out = pl.BlockSpec((rows, local, width), lambda p, own: (0, 0, 0))
    results = pl.pallas_call(
        functools.partial(attend_back_kernel, team, rows, local, block, unroll, experts),
        grid_spec=pltpu.PrefetchScalarGridSpec(
            num_scalar_prefetch=1,
            grid=(pairs,),
            in_specs=[fixed(rows, local, width)] * team
            + [fixed(length, width), weight(0), weight(1), weight(2)]
            + [pl.BlockSpec((PAIR, width), lambda p, own: (own[1] * pairs + p, 0))]
            + [fixed(1, length), columns(), columns(), columns(), across, logs],
            out_specs=[out] * team
            + [pl.BlockSpec((experts, 4, width // experts, PAIR), lambda p, own: (0, 0, 0, p))],
            scratch_shapes=[
                pltpu.VMEM((length, width), LOW),
                pltpu.VMEM((length, PAIR), LOW),
                pltpu.VMEM((PAIR, length), LOW),
                pltpu.VMEM((2, length), FULL),
                pltpu.VMEM((PAIR, length), FULL),
                pltpu.VMEM((length, 3 * PAIR), LOW),
                pltpu.VMEM((length, width), FULL),
            ],
        ),
        out_shape=[shape((rows, local, width), LOW)] * team
        + [shape((experts, 4, width // experts, share), LOW)],
        compiler_params=pltpu.CompilerParams(vmem_limit_bytes=VMEM_LIMIT),
        cost_estimate=pl.CostEstimate(
            flops=4 * length * width * 4 * share + 20 * length * length * share,
            bytes_accessed=6 * length * width + 24 * length * share,
            transcendentals=length * length * pairs,
        ),
        name="attend_back",
    )(own, *pieces, x, weights, weights, weights, out_weights, low, q, k, v, ot, logs_in)
    return results[team], results[:team]


GELU_SCALE = math.sqrt(2.0 / math.pi)
GELU_CUBE = 0.044715


def expert_kernel(count, first, last, own_ref, *refs):
    x_refs, refs = refs[:count], refs[count:]
    g_refs, refs = refs[:count], refs[count:]
    up_ref, down_ref, refs = refs[0], refs[1], refs[2:]
    if not first:
        y_in, gx_in, refs = refs[0], refs[1], refs[2:]
    gup_ref, gdown_ref, refs = refs[0], refs[1], refs[2:]
    if last:
        y_out, gx_out, y_sum, gx_sum, refs = refs[0], refs[1], refs[2], refs[3], refs[4:]
    else:
        y_sum, gx_sum, refs = refs[0], refs[1], refs[2:]
    x_ref, g_ref = refs
    step = pl.program_id(0)
    size = x_refs[0].shape[0]

    @pl.when(step == 0)
    def _():
        for index in range(count):
            span = pl.ds(index * size, size)
            x_ref[span, :] = x_refs[index][...]
            g_ref[span, :] = g_refs[index][...]
        if first:
            y_sum[...] = jnp.zeros_like(y_sum)
            gx_sum[...] = jnp.zeros_like(gx_sum)
        else:
            y_sum[...] = y_in[...]
            gx_sum[...] = gx_in[...]

    x = x_ref[...]
    g = g_ref[...]
    inner = dot(x, up_ref[...])
    square = inner * inner
    curve = jnp.tanh(GELU_SCALE * inner * (1.0 + GELU_CUBE * square))
    half = 0.5 + 0.5 * curve
    active = (inner * half).astype(LOW)
    slope = half + (0.5 * GELU_SCALE) * inner * (1.0 - curve * curve) * (
        1.0 + (3.0 * GELU_CUBE) * square
    )
    grad_inner = (dot(g, down_ref[...], NT) * slope).astype(LOW)
    gdown_ref[...] = dot(active, g, TN).astype(LOW)
    gup_ref[...] = dot(x, grad_inner, TN).astype(LOW)
    y_sum[...] += dot(active, down_ref[...])
    gx_sum[...] += dot(grad_inner, up_ref[...], NT)

    if last:

        @pl.when(step == pl.num_programs(0) - 1)
        def _():
            for index in range(count):
                span = pl.ds(index * size, size)
                y_out[own_ref[2] ^ index] = y_sum[span, :].astype(LOW)
                gx_out[own_ref[2] ^ index] = gx_sum[span, :].astype(LOW)


def expert(own, xs, gs, up, down, part, parts, sums):
    count = len(xs)
    size, width = xs[0].shape
    hidden = up.shape[1] // parts
    block = math.gcd(hidden, 512)
    steps = hidden // block
    first, last = part == 0, part == parts - 1
    rows = pl.BlockSpec((size, width), lambda f, own: (0, 0))
    whole = pl.BlockSpec((count * size, width), lambda f, own: (0, 0))
    every = pl.BlockSpec((count, size, width), lambda f, own: (0, 0, 0))
    shape = jax.ShapeDtypeStruct
    sum_shape = shape((count * size, width), FULL)
    in_specs = [rows] * (2 * count) + [
        pl.BlockSpec((width, block), lambda f, own: (0, f + part * steps)),
        pl.BlockSpec((block, width), lambda f, own: (f + part * steps, 0)),
    ]
    out_specs = [
        pl.BlockSpec((width, block), lambda f, own: (0, f)),
        pl.BlockSpec((block, width), lambda f, own: (f, 0)),
    ]
    out_shape = [shape((width, hidden), LOW), shape((hidden, width), LOW)]
    scratch = []
    if not first:
        in_specs += [whole] * 2
    if last:
        out_specs += [every] * 2
        out_shape += [shape((count, size, width), LOW)] * 2
        scratch += [pltpu.VMEM(sum_shape.shape, FULL)] * 2
    else:
        out_specs += [whole] * 2
        out_shape += [sum_shape] * 2
    results = pl.pallas_call(
        functools.partial(expert_kernel, count, first, last),
        grid_spec=pltpu.PrefetchScalarGridSpec(
            num_scalar_prefetch=1,
            grid=(steps,),
            in_specs=in_specs,
            out_specs=out_specs,
            scratch_shapes=scratch + [pltpu.VMEM((count * size, width), LOW)] * 2,
        ),
        out_shape=out_shape,
        compiler_params=pltpu.CompilerParams(vmem_limit_bytes=VMEM_LIMIT),
        cost_estimate=pl.CostEstimate(
            flops=12 * count * size * width * hidden,
            bytes_accessed=8 * width * hidden + 8 * count * size * width,
            transcendentals=count * size * hidden,
        ),
        name="expert",
    )(own, *xs, *gs, up, down, *sums)
    return results[0], results[1], results[2:]


def tie(values, others):
    count, total = len(values), len(values) + len(others)
    return pl.pallas_call(
        lambda *refs: None,
        in_specs=[pl.BlockSpec(memory_space=pl.ANY)] * total,
        out_specs=[pl.BlockSpec(memory_space=pl.ANY)] * count,
        out_shape=[jax.ShapeDtypeStruct(value.shape, value.dtype) for value in values],
        input_output_aliases={index: index for index in range(count)},
        name="tie",
    )(*values, *others)


def put_kernel(count, joined, place, own_ref, *refs):
    out_ref = refs[count + joined]
    size, cut, _ = refs[0].shape
    for i in range(count):
        for n in range(size):
            first = pl.multiple_of(place(own_ref, i, n) * cut, cut)
            out_ref[pl.ds(first, cut), :] = refs[i][n].astype(FULL)


def put_chunk(own, parts, into, shape, block, place):
    count, (size, cut, width) = len(parts), parts[0].shape
    joined = [] if into is None else [into]
    return pl.pallas_call(
        functools.partial(put_kernel, count, len(joined), place),
        grid_spec=pltpu.PrefetchScalarGridSpec(
            num_scalar_prefetch=1,
            grid=(1,),
            in_specs=[pl.BlockSpec((size, cut, width), lambda s, own: (0, 0, 0))] * count
            + [pl.BlockSpec(memory_space=pl.ANY)] * len(joined),
            out_specs=pl.BlockSpec((count * size * cut, width), lambda s, own: block),
        ),
        out_shape=jax.ShapeDtypeStruct(shape, FULL),
        input_output_aliases={1 + count: 0} if joined else {},
        compiler_params=pltpu.CompilerParams(vmem_limit_bytes=VMEM_LIMIT),
        cost_estimate=pl.CostEstimate(
            flops=0, bytes_accessed=8 * count * size * cut * width, transcendentals=0
        ),
        name="put_chunk",
    )(own, *parts, *joined)


def place_kernel(team, rows, experts, own_ref, *refs):
    parts, (qkv_ref, out_ref, hold_ref) = refs[: team * experts], refs[team * experts :]
    cut, share = parts[0].shape[2:]
    which = pl.program_id(0)

    def rows_of(m, k):
        index = (own_ref[2] ^ m) * rows + k
        return pl.ds(pl.multiple_of(index * cut, cut), cut)

    for j in range(team):
        member = lax.rem(own_ref[1] + (team - j), team)
        span = pl.ds(pl.multiple_of(member * share, share), share)

        @pl.when(which < 3)
        def _():
            for m in range(experts):
                for k in range(rows):
                    part = parts[m * team + j][k, 0]
                    qkv_ref[rows_of(m, k), span] = part.astype(FULL)

        @pl.when(which == 3)
        def _():
            for m in range(experts):
                for k in range(rows):
                    part = parts[m * team + j][k, 0]
                    hold_ref[rows_of(m, k), :] = part.astype(FULL)
            out_ref[span, :] = hold_ref[...].T


def place_weights(own, parts, team, rows, experts):
    _, _, cut, share = parts[0].shape
    width, padded = experts * rows * cut, team * share
    return pl.pallas_call(
        functools.partial(place_kernel, team, rows, experts),
        grid_spec=pltpu.PrefetchScalarGridSpec(
            num_scalar_prefetch=1,
            grid=(4,),
            in_specs=[pl.BlockSpec((rows, 1, cut, share), lambda w, own: (0, w, 0, 0))]
            * (team * experts),
            out_specs=[
                pl.BlockSpec((width, padded), lambda w, own: (0, jnp.minimum(w, 2))),
                pl.BlockSpec((padded, width), lambda w, own: (0, 0)),
            ],
            scratch_shapes=[pltpu.VMEM((width, share), FULL)],
        ),
        out_shape=[
            jax.ShapeDtypeStruct((width, 3 * padded), FULL),
            jax.ShapeDtypeStruct((padded, width), FULL),
        ],
        compiler_params=pltpu.CompilerParams(vmem_limit_bytes=VMEM_LIMIT),
        cost_estimate=pl.CostEstimate(
            flops=0, bytes_accessed=24 * width * padded, transcendentals=0
        ),
        name="place_weights",
    )(own, *parts)


def norm_back_kernel(team, own_ref, *refs):
    parts, refs = refs[:team], refs[team:]
    x_ref, more_ref, gain_ref, out_ref, sum_ref = refs
    unit, inverse = standard(x_ref[0].astype(FULL))
    grad = parts[0][0].astype(FULL)
    for part in parts[1:]:
        grad = grad + part[0].astype(FULL)
    back, gain, bias = standard_back(grad, gain_ref[...], unit, inverse)
    out_ref[0] = (back + more_ref[0].astype(FULL)).astype(LOW)

    @pl.when(pl.program_id(0) == 0)
    def _():
        sum_ref[...] = jnp.zeros_like(sum_ref)

    sum_ref[0:1, :] += gain[None]
    sum_ref[1:2, :] += bias[None]


def norm_back(own, parts, x, more, gain):
    rows, local, width = x.shape
    block = pl.BlockSpec((1, local, width), lambda k, own: (k, 0, 0))
    home = lambda k, own: (lax.rem(own[0] + (rows - k), rows), 0, 0)
    return pl.pallas_call(
        functools.partial(norm_back_kernel, len(parts)),
        grid_spec=pltpu.PrefetchScalarGridSpec(
            num_scalar_prefetch=1,
            grid=(rows,),
            in_specs=[block] * (len(parts) + 2)
            + [pl.BlockSpec((1, width), lambda k, own: (0, 0))],
            out_specs=[
                pl.BlockSpec((1, local, width), home),
                pl.BlockSpec((8, width), lambda k, own: (0, 0)),
            ],
        ),
        out_shape=[
            jax.ShapeDtypeStruct(x.shape, LOW),
            jax.ShapeDtypeStruct((8, width), FULL),
        ],
        cost_estimate=pl.CostEstimate(flops=0, bytes_accessed=40 * x.size, transcendentals=0),
        name="norm_back",
    )(own, *parts, x, more, gain[None])


def add_low(a, b):
    return (a.astype(FULL) + b.astype(FULL)).astype(LOW)


def pick(value, index):
    return lax.dynamic_index_in_dim(value, index, 0, keepdims=False)


def ring_scatter(value, size, place, send):
    total = pick(value, (place + size - 1) % size)
    for step in range(size - 1):
        total = add_low(send(total), pick(value, (place + 2 * size - 2 - step) % size))
    return total


def ring_gather(value, size, place, send):
    out = jnp.zeros((size,) + value.shape, value.dtype)
    out = lax.dynamic_update_index_in_dim(out, value, place, 0)
    for step in range(size - 1):
        value = send(value)
        out = lax.dynamic_update_index_in_dim(out, value, (place + size - 1 - step) % size, 0)
    return out


def per_device(
    block_input, segment_ids, expert_ids, ln1_gain, ln1_bias, ln2_gain, ln2_bias,
    w_qkv, w_attn_out, w_in, w_down, grad_out,
):
    rows, local, width = block_input.shape
    seq = lax.axis_size("seq")
    experts = lax.axis_size("ex")
    team = seq // rows
    length = seq * local
    owned = rows * local
    pairs = -(-HEADS // (2 * team))
    share = pairs * PAIR
    padded = share * team
    place = lax.axis_index("seq")
    mine = lax.axis_index("ex")
    row, member = place // team, place % team
    slots = rows * MOST

    def row_send(value, k):
        if k % rows == 0:
            return value
        pattern = [(a * team + b, (a + k) % rows * team + b) for a in range(rows) for b in range(team)]
        return lax.ppermute(value, "seq", pattern)

    def team_send(value, j):
        if j % team == 0:
            return value
        pattern = [(a * team + b, a * team + (b + j) % team) for a in range(rows) for b in range(team)]
        return lax.ppermute(value, "seq", pattern)

    def swap(value, axis, m):
        if m == 0 or m >= lax.axis_size(axis):
            return value
        return lax.ppermute(value, axis, [(a, a ^ m) for a in range(lax.axis_size(axis))])

    across_rows = [[r * team + g for r in range(rows)] for g in range(team)]

    def swap_rows(value):
        return lax.all_to_all(value, "seq", 0, 0, tiled=True, axis_index_groups=across_rows)

    def swap_experts(value):
        return lax.all_to_all(value, "ex", 0, 0, tiled=True)

    center = (block_input - jnp.mean(block_input, -1, keepdims=True)).astype(LOW)
    owned_x = [row_send(pick(center, (row + k) % rows), k) for k in range(rows)]
    pieces = [team_send(piece, j) for j in range(team) for piece in owned_x]

    labels = jnp.pad(expert_ids.reshape(rows, 1, local), ((0, 0), (0, 15), (0, width - local)))
    carried = jnp.concatenate([grad_out.astype(LOW), labels.astype(LOW)], 1)
    carried = tie([carried], [owned_x[1]])[0]
    owned_g = jnp.stack([row_send(pick(carried, (row + k) % rows), k) for k in range(rows)])
    grad_low = owned_g[:, :local]
    chosen = owned_g[:, local, :local].astype(jnp.int32)

    segments = lax.dynamic_slice_in_dim(segment_ids, row, 1, 0)[0]
    lows = jnp.sum((segments[:, None] < segments[None, :]).astype(jnp.int32), 0)[None, :]

    weights, out_weights = w_qkv, w_attn_out
    if padded != width:
        extra = padded - width
        weights = jnp.pad(w_qkv.reshape(width, 3, width), ((0, 0), (0, 0), (0, extra)))
        weights = weights.reshape(width, 3 * padded)
        out_weights = jnp.pad(w_attn_out, ((0, extra), (0, 0)))

    own = jnp.stack([row, member, mine]).astype(jnp.int32)
    results = attend(own, pieces, ln1_gain, ln1_bias, weights, lows, team, rows, pairs)
    full, q, k, v, ot, logs = results[:6]
    branch = 0.0
    for j, part in enumerate(tie(results[6:], [owned_g])):
        first = (member + team - j) % team * share
        weight = lax.dynamic_slice_in_dim(out_weights, first, share, 0)
        branch = branch + dot(team_send(part, j).reshape(owned, share), weight)

    residual = jnp.concatenate(owned_x, 0).astype(FULL)
    middle = residual + branch
    unit_two, inverse_two = standard(middle)
    normed_two = (unit_two * ln2_gain + ln2_bias).astype(LOW)

    relative = chosen ^ mine
    onehot = (relative[..., None] == jnp.arange(experts, dtype=jnp.int32)).astype(jnp.int32)
    rank = jnp.cumsum(onehot, 1) - onehot
    target = relative * MOST + jnp.sum(rank * onehot, -1)
    numbers = jnp.arange(experts * MOST, dtype=jnp.int32)[None, :, None]

    def routes(target):
        match = (target[:, None, :] == numbers).astype(LOW)
        return match.reshape(rows, experts, MOST, local)

    route = routes(target)
    back_route = routes((target // MOST ^ mine) * MOST + target % MOST)
    named = (chosen[..., None] == jnp.arange(experts, dtype=jnp.int32)).astype(FULL)
    counts = jnp.sum(named, (0, 1))

    def dispatch(value):
        placed = jnp.einsum(
            "remt,rtd->ermd", route, value.reshape(rows, local, width), preferred_element_type=FULL
        )
        placed = placed.astype(LOW).reshape(experts, slots, width)
        return [swap(placed[m], "ex", m) for m in range(experts)]

    def collect(returned):
        return jnp.einsum(
            "remt,ermd->rtd",
            back_route,
            returned.reshape(experts, rows, MOST, width),
            preferred_element_type=FULL,
        ).reshape(owned, width)

    grad_arrived = dispatch(grad_low)
    arrived = dispatch(normed_two)

    hops = rows - 1

    def along_team(value):
        return team_send(value, 1)

    def team_scatter(value):
        return ring_scatter(value, team, member, along_team)

    def team_gather(value):
        return [team_send(value, j) for j in range(team)]

    def cut_up(value, sizes):
        return value.reshape(sizes + (value.shape[0] // seq,) + value.shape[1:])

    def first_hop(value):
        return row_send(pick(value, (row + rows - 1) % rows), 1)

    def joined(came, value, step):
        return add_low(came, pick(value, (row + 2 * rows - 2 - step) % rows))

    def next_hop(came, value, step):
        return row_send(joined(came, value, step), 1)

    def sync(*values):
        leaves, tree = jax.tree.flatten(values)
        return jax.tree.unflatten(tree, tie(leaves, []))

    def team_first(own_ref, i, n):
        device = lax.rem(own_ref[1] + (team - i), team)
        return device * rows + lax.rem(own_ref[0] + (rows - n), rows)

    def rows_first(own_ref, i, n):
        device = lax.rem(own_ref[1] + (team - n), team)
        return lax.rem(own_ref[0] + (rows - i), rows) * team + device

    up_shape, down_shape = w_in.shape[1:], w_down.shape[1:]

    up_one, down_one, sums = expert(own, arrived, grad_arrived, w_in[0], w_down[0], 0, 2, ())
    cut_a = cut_up(up_one, (team, rows))
    cut_z = cut_up(down_one, (rows, team))
    half_a = team_scatter(cut_a)
    z = first_hop(cut_z)
    up_two, down_two, sums = expert(own, arrived, grad_arrived, w_in[0], w_down[0], 1, 2, sums)
    produced, grad_rows = sums
    z, produced, grad_rows = sync(z, produced, grad_rows)

    grad_rows = swap_experts(grad_rows)
    z = next_hop(z, cut_z, 0)
    grad_rows, produced, half_a = sync(grad_rows, produced, half_a)

    produced = swap_experts(produced)
    back_two, grad_gain_two, grad_bias_two = standard_back(
        collect(grad_rows), ln2_gain, unit_two, inverse_two
    )
    grad_branch = (back_two + grad_low.reshape(owned, width).astype(FULL)).astype(LOW)
    grad_branch = grad_branch.reshape(rows, local, width)
    grad_branch, z = sync(grad_branch, z)

    branches = [team_send(grad_branch, j) for j in range(team)]
    z = next_hop(z, cut_z, 1)
    half_a, up_two, down_two = sync(half_a, up_two, down_two)

    a = first_hop(half_a)
    half_b = team_scatter(cut_up(up_two, (team, rows)))
    z, produced = sync(z, produced)

    z = joined(z, cut_z, 2)
    change = (branch + collect(produced)).astype(LOW).reshape(rows, local, width)
    change = jnp.stack([change[(rows - n) % rows] for n in range(rows)] * 2)
    change = lax.dynamic_slice_in_dim(change, (rows - row) % rows, rows, 0)
    a, change = sync(a, change)

    a = next_hop(a, half_a, 0)
    a, branches, down_two, change = sync(a, branches, down_two, change)

    a = next_hop(a, half_a, 1)
    change = swap_rows(change)
    half_c = team_scatter(cut_up(down_two, (team, rows)))
    grads, grad_full = attend_back(
        own, branches, full, weights, out_weights, lows, q, k, v, ot, logs,
        team, rows, pairs, experts,
    )
    half_b, a, z, grads, grad_full = sync(half_b, a, z, grads, grad_full)

    grads = swap_experts(grads)
    grad_full = [team_send(part, j) for j, part in enumerate(grad_full)]
    b = first_hop(half_b)
    a = joined(a, half_a, 2)
    change, half_c, a, z = sync(change, half_c, a, z)

    pieces_a = [a, row_send(a, 1)]
    z = team_scatter(z)
    block_output = block_input + change.astype(FULL)
    b, block_output = sync(b, block_output)

    b = next_hop(b, half_b, 0)
    pieces_a = sync(pieces_a)[0]

    pieces_a = pieces_a + [row_send(pieces_a[-1], 1)]
    b, grads = sync(b, grads)

    b = next_hop(b, half_b, 1)
    cut = width // (experts * rows)
    grads = jnp.sum(grads.astype(FULL), 0).astype(LOW).reshape(4, rows, cut, share)
    grads = swap_rows(grads.swapaxes(0, 1))
    pieces_a, grad_full = sync(pieces_a, grad_full)

    pieces_a = pieces_a + [row_send(pieces_a[-1], 1)]
    grad_change, norm_sums = norm_back(
        own, grad_full, jnp.stack(owned_x), back_two.reshape(rows, local, width), ln1_gain
    )
    b, z, grad_change, norm_sums = sync(b, z, grad_change, norm_sums)

    b = joined(b, half_b, 2)
    pieces_b = [b, row_send(b, 1)]
    z = jnp.stack(team_gather(z))
    small = jnp.stack(
        [
            norm_sums[0], norm_sums[1], grad_gain_two, grad_bias_two,
            jnp.pad(counts, (0, width - experts)),
        ]
    )
    small = small + swap(small, "ex", 1)
    pieces_a, half_c = sync(pieces_a, half_c)

    c = first_hop(half_c)
    all_a = team_gather(jnp.stack(pieces_a))
    pieces_b, grads = sync(pieces_b, grads)

    pieces_b = pieces_b + [row_send(pieces_b[-1], 1)]
    grads = jnp.sum(grads.astype(FULL), 0).astype(LOW)
    grads = swap_rows(jnp.broadcast_to(grads[None], (rows,) + grads.shape))
    c, small = sync(c, small)

    c = next_hop(c, half_c, 0)
    small = small + swap(small, "ex", 2)
    pieces_b = sync(pieces_b)[0]

    pieces_b = pieces_b + [row_send(pieces_b[-1], 1)]
    c, z = sync(c, z)

    c = next_hop(c, half_c, 1)
    pieces_b, grads, all_a = sync(pieces_b, grads, all_a)

    share_grads = team_gather(grads)
    all_b = team_gather(jnp.stack(pieces_b))
    pieces_z = [z, row_send(z, 1)]
    grad_up = put_chunk(own, all_a, None, up_shape, (0, 0), team_first)
    c, small, grad_up = sync(c, small, grad_up)

    c = joined(c, half_c, 2)
    pieces_c = [c, row_send(c, 1)]
    small = small + swap(small, "seq", 1)
    pieces_z = sync(pieces_z)[0]

    pieces_z = pieces_z + [row_send(pieces_z[-1], 1)]
    pieces_c, share_grads = sync(pieces_c, share_grads)

    pieces_c = pieces_c + [row_send(pieces_c[-1], 1)]
    far_grads = [swap(part, "ex", 2) for part in share_grads]
    pieces_z, small, grad_change = sync(pieces_z, small, grad_change)

    pieces_z = pieces_z + [row_send(pieces_z[-1], 1)]
    small = small + swap(small, "seq", 2)
    pieces_c, all_b, far_grads, share_grads = sync(pieces_c, all_b, far_grads, share_grads)

    pieces_c = pieces_c + [row_send(pieces_c[-1], 1)]
    near = [swap(part, "ex", 1) for part in share_grads]
    far = [swap(part, "ex", 1) for part in far_grads]
    grad_up = put_chunk(own, all_b, grad_up, up_shape, (0, 1), team_first)
    pieces_z, small, grad_up = sync(pieces_z, small, grad_up)

    grad_change = swap_rows(grad_change)
    for bit in range(2, seq.bit_length() - 1):
        small = small + swap(small, "seq", 1 << bit)
    pieces_c, near, far, share_grads, far_grads = sync(
        pieces_c, near, far, share_grads, far_grads
    )

    all_c = team_gather(jnp.stack(pieces_c))
    parts = share_grads + near + far_grads + far
    grad_qkv, grad_attn_out = place_weights(own, parts, team, rows, experts)
    grad_down = put_chunk(own, pieces_z, None, down_shape, (0, 0), rows_first)
    grad_input = grad_out + grad_change.astype(FULL)
    all_c, grad_qkv, grad_input, grad_down = sync(all_c, grad_qkv, grad_input, grad_down)

    if padded != width:
        grad_qkv = grad_qkv.reshape(width, 3, padded)[..., :width].reshape(width, 3 * width)
        grad_attn_out = grad_attn_out[:width]
    grad_down = put_chunk(own, all_c, grad_down, down_shape, (1, 0), team_first)
    load = small[4, :experts] * (experts / (rows * length * experts))
    return (
        block_output, grad_input, grad_qkv, grad_attn_out, small[0], small[1], small[2],
        small[3], grad_up[None], grad_down[None], load,
    )


def solution(mesh):
    tokens = P("ex", "seq", None)
    expert_axis = P("ex", None, None)
    return jax.shard_map(
        per_device,
        mesh=mesh,
        in_specs=(
            tokens, P("ex", None), tokens, P(), P(), P(), P(), P(), P(),
            expert_axis, expert_axis, tokens,
        ),
        out_specs=(
            tokens, tokens, P(), P(), P(), P(), P(), P(), expert_axis, expert_axis, P(),
        ),
        check_vma=False,
    )
```

```python
import functools
import math

import jax
import jax.numpy as jnp
from jax import lax
from jax.experimental import pallas as pl
from jax.experimental.pallas import tpu as pltpu
from jax.sharding import PartitionSpec as P

HEADS = 12
HEAD = 64
MOST = 48
PAIR = 2 * HEAD
EPSILON = 1e-05
NEGATIVE = -1e30
LOW = jnp.bfloat16
FULL = jnp.float32
VMEM_LIMIT = 60 * 1024 * 1024
NN = (((1,), (0,)), ((), ()))
NT = (((1,), (1,)), ((), ()))
TN = (((0,), (0,)), ((), ()))


def dot(a, b, dims=NN):
    return lax.dot_general(a, b, dims, preferred_element_type=FULL)


def loop(first, last, unroll, body, carry):
    if unroll:
        for index in range(first, last):
            carry = body(index, carry)
        return carry
    return lax.fori_loop(first, last, body, carry)


def each(count, unroll, body):
    def step(index, carry):
        body(index)
        return carry

    loop(0, count, unroll, step, 0)


def tile_mask(shape, low_row, key_first, query_first, diagonal):
    key_pos = key_first + lax.broadcasted_iota(jnp.int32, shape, 0)
    allowed = key_pos >= low_row
    if diagonal:
        query_pos = query_first + lax.broadcasted_iota(jnp.int32, shape, 1)
        allowed = allowed & (key_pos <= query_pos)
    return allowed


def head_lanes(value, head):
    lane = lax.broadcasted_iota(jnp.int32, value.shape, 1)
    return jnp.where((lane // HEAD) == head, value, jnp.zeros_like(value))


def place_of(own_ref, j, k, team, rows, local):
    row = lax.rem(own_ref[0] + (rows - k), rows)
    member = lax.rem(own_ref[1] + (team + j) % team, team)
    return pl.ds(pl.multiple_of((row * team + member) * local, local), local)


def standard(value):
    center = value - jnp.mean(value, -1, keepdims=True)
    spread = jnp.mean(center * center, -1, keepdims=True)
    inverse = lax.rsqrt(spread + EPSILON)
    return center * inverse, inverse


def standard_back(grad, gain, unit, inverse):
    u = grad * gain
    lean = jnp.mean(u * unit, -1, keepdims=True)
    back = (u - jnp.mean(u, -1, keepdims=True) - unit * lean) * inverse
    return back, jnp.sum(grad * unit, 0), jnp.sum(grad, 0)


def attend_kernel(team, rows, local, block, unroll, own_ref, *refs):
    pieces, refs = refs[: team * rows], refs[team * rows :]
    gain_ref, bias_ref, wq_ref, wk_ref, wv_ref, low_ref = refs[:6]
    x_ref, q_ref, k_ref, v_ref, ot_ref, log_ref = refs[6:12]
    o_refs = refs[12 : 12 + team]
    vt_ref, o_ref = refs[12 + team :]
    length = x_ref.shape[0]
    count = length // block

    @pl.when(pl.program_id(0) == 0)
    def _():
        for j in range(team):
            for k in range(rows):
                unit, _ = standard(pieces[j * rows + k][...].astype(FULL))
                normed = unit * gain_ref[...] + bias_ref[...]
                x_ref[place_of(own_ref, -j, k, team, rows, local), :] = normed.astype(LOW)

    weight = jnp.concatenate([wq_ref[...], wk_ref[...], wv_ref[...]], 1)

    def project(index):
        span = pl.ds(index * block, block)
        both = dot(x_ref[span, :], weight).astype(LOW)
        q_ref[span, :] = both[:, :PAIR] * LOW(HEAD**-0.5)
        k_ref[span, :] = both[:, PAIR : 2 * PAIR]
        v = both[:, 2 * PAIR :]
        v_ref[span, :] = v
        vt_ref[:, span] = v.T

    each(count, unroll, project)

    def one_block(qi):
        span = pl.ds(qi * block, block)
        low_row = low_ref[:, span]
        q = q_ref[span, :]

        def scores_of(head, first, size, diagonal):
            scores = dot(k_ref[pl.ds(first, size), :], head_lanes(q, head), NT)
            allowed = tile_mask((size, block), low_row, first, qi * block, diagonal)
            return jnp.where(allowed, scores, NEGATIVE)

        def summed_of(head, first, size, weights):
            values = vt_ref[pl.ds(head * HEAD, HEAD), pl.ds(first, size)]
            return dot(values, weights.astype(LOW))

        def at_once(head):
            spans = [(0, qi * block, False), (qi * block, block, True)]
            spans = [(first, size, last) for first, size, last in spans if size]
            tiles = [scores_of(head, *part) for part in spans]
            high = functools.reduce(
                jnp.maximum, [jnp.max(tile, 0, keepdims=True) for tile in tiles]
            )
            tiles = [jnp.exp(tile - high) for tile in tiles]
            total = sum(jnp.sum(tile, 0, keepdims=True) for tile in tiles)
            summed = sum(
                summed_of(head, first, size, tile) for (first, size, _), tile in zip(spans, tiles)
            )
            return high, total, summed

        def in_turn(head):
            def step(kj, state, diagonal):
                scores = scores_of(head, kj * block, block, diagonal)
                high = jnp.max(scores, 0, keepdims=True)
                if state is not None:
                    high = jnp.maximum(high, state[0])
                weights = jnp.exp(scores - high)
                total = jnp.sum(weights, 0, keepdims=True)
                summed = summed_of(head, kj * block, block, weights)
                if state is not None:
                    fade = jnp.exp(state[0] - high)
                    total, summed = total + state[1] * fade, summed + state[2] * fade
                return high, total, summed

            return lax.fori_loop(
                0, qi, lambda kj, state: step(kj, state, False), step(qi, None, True)
            )

        done = []
        for head in range(2):
            high, total, summed = at_once(head) if unroll else in_turn(head)
            log_ref[0, pl.ds(head, 1), span] = high + jnp.log(total)
            done.append(summed / total)
        both = jnp.concatenate(done, 0)
        ot_ref[:, span] = both
        o_ref[span, :] = both.T.astype(LOW)

    each(count, unroll, one_block)
    for j in range(team):
        for k in range(rows):
            o_refs[j][k] = o_ref[place_of(own_ref, j, k, team, rows, local), :]


def attend_back_kernel(team, rows, local, block, unroll, experts, own_ref, *refs):
    pieces, refs = refs[:team], refs[team:]
    x_ref, wq_ref, wk_ref, wv_ref, wo_ref, low_ref = refs[:6]
    q_ref, k_ref, v_ref, ot_ref, log_ref = refs[6:11]
    gx_refs, refs = refs[11 : 11 + team], refs[11 + team :]
    gw_ref, b_ref, g_ref, kt_ref, delta_ref, dqt_ref, d_ref, sum_ref = refs
    length, width = x_ref.shape
    count = length // block
    scale = HEAD**-0.5
    pair = pl.program_id(0)

    @pl.when(pair == 0)
    def _():
        for j in range(team):
            for k in range(rows):
                b_ref[place_of(own_ref, -j, k, team, rows, local), :] = pieces[j][k]
        sum_ref[...] = jnp.zeros_like(sum_ref)

    def prepare(index):
        span = pl.ds(index * block, block)
        kt_ref[:, span] = k_ref[span, :].T
        g = dot(b_ref[span, :], wo_ref[...], NT).astype(LOW)
        g_ref[span, :] = g
        product = g.astype(FULL).T * ot_ref[:, span]
        for head in range(2):
            part = product[head * HEAD : (head + 1) * HEAD]
            delta_ref[pl.ds(head, 1), span] = jnp.sum(part, 0, keepdims=True)
        dqt_ref[:, span] = jnp.zeros((PAIR, block), FULL)

    each(count, unroll, prepare)

    def one_block(kj):
        keys = pl.ds(kj * block, block)
        k = k_ref[keys, :]
        v = v_ref[keys, :]

        def tile(qi, carry, diagonal):
            grad_k, grad_v = carry
            span = pl.ds(qi * block, block)
            q = q_ref[span, :]
            g = g_ref[span, :]
            allowed = tile_mask(
                (block, block), low_ref[:, span], kj * block, qi * block, diagonal
            )
            for head in range(2):
                qm = head_lanes(q, head)
                gm = head_lanes(g, head)
                part = pl.ds(head * HEAD, HEAD)
                probs = jnp.exp(dot(k, qm, NT) - log_ref[0, pl.ds(head, 1), span])
                probs = jnp.where(allowed, probs, 0.0)
                grad_probs = dot(v, gm, NT)
                grad_scores = (probs * (grad_probs - delta_ref[pl.ds(head, 1), span])).astype(LOW)
                grad_v = grad_v + dot(probs.astype(LOW), gm)
                grad_k = grad_k + dot(grad_scores, qm)
                dqt_ref[part, span] += dot(kt_ref[part, keys], grad_scores)
            return grad_k, grad_v

        zero = jnp.zeros((block, PAIR), FULL)
        grad_k, grad_v = loop(
            kj + 1,
            count,
            unroll,
            lambda qi, carry: tile(qi, carry, False),
            tile(kj, (zero, zero), True),
        )
        d_ref[keys, PAIR : 2 * PAIR] = grad_k.astype(LOW)
        d_ref[keys, 2 * PAIR :] = grad_v.astype(LOW)

    each(count, unroll, one_block)

    weight = jnp.concatenate([wq_ref[...], wk_ref[...], wv_ref[...]], 1)

    def spread(index):
        span = pl.ds(index * block, block)
        d_ref[span, :PAIR] = (dqt_ref[:, span] * scale).T.astype(LOW)
        sum_ref[span, :] += dot(d_ref[span, :], weight, NT)

    each(count, unroll, spread)

    grads = dot(x_ref[...], d_ref[...], TN).astype(LOW)
    out_grads = dot(ot_ref[...].astype(LOW), b_ref[...]).T.astype(LOW)
    cut = width // experts
    for e in range(experts):
        span = slice(e * cut, (e + 1) * cut)
        for which in range(3):
            gw_ref[e, which] = grads[span, which * PAIR : (which + 1) * PAIR]
        gw_ref[e, 3] = out_grads[span]

    @pl.when(pair == pl.num_programs(0) - 1)
    def _():
        for j in range(team):
            for k in range(rows):
                gx_refs[j][k] = sum_ref[place_of(own_ref, j, k, team, rows, local), :].astype(LOW)


def fixed(*shape):
    return pl.BlockSpec(shape, lambda p, own: (0,) * len(shape), pipeline_mode=pl.Buffered(1))


def attention_specs(length, width, pairs, all_pairs):
    weight = lambda which: pl.BlockSpec(
        (width, PAIR), lambda p, own: (0, which * all_pairs + own[1] * pairs + p)
    )
    columns = lambda: pl.BlockSpec((length, PAIR), lambda p, own: (0, p))
    across = pl.BlockSpec((PAIR, length), lambda p, own: (p, 0))
    logs = pl.BlockSpec((1, 2, length), lambda p, own: (p, 0, 0))
    return weight, columns, across, logs


def attend(own, pieces, gain, bias, weights, low, team, rows, pairs):
    local, width = pieces[0].shape
    length = team * rows * local
    share = pairs * PAIR
    block = math.gcd(length, 512)
    unroll = length // block <= 4
    weight, columns, across, logs = attention_specs(length, width, pairs, pairs * team)
    shape = jax.ShapeDtypeStruct
    return pl.pallas_call(
        functools.partial(attend_kernel, team, rows, local, block, unroll),
        grid_spec=pltpu.PrefetchScalarGridSpec(
            num_scalar_prefetch=1,
            grid=(pairs,),
            in_specs=[fixed(local, width)] * len(pieces)
            + [fixed(1, width)] * 2
            + [weight(0), weight(1), weight(2), fixed(1, length)],
            out_specs=[pl.BlockSpec((length, width), lambda p, own: (0, 0))]
            + [columns(), columns(), columns(), across, logs]
            + [pl.BlockSpec((rows, local, PAIR), lambda p, own: (0, 0, p))] * team,
            scratch_shapes=[pltpu.VMEM((PAIR, length), LOW), pltpu.VMEM((length, PAIR), LOW)],
        ),
        out_shape=[shape((length, width), LOW)]
        + [shape((length, share), LOW)] * 3
        + [shape((share, length), FULL), shape((pairs, 2, length), FULL)]
        + [shape((rows, local, share), LOW)] * team,
        compiler_params=pltpu.CompilerParams(vmem_limit_bytes=VMEM_LIMIT),
        cost_estimate=pl.CostEstimate(
            flops=2 * length * width * 3 * share + 8 * length * length * share,
            bytes_accessed=4 * length * width + 12 * length * share,
            transcendentals=length * length * pairs,
        ),
        name="attend",
    )(own, *pieces, gain[None], bias[None], weights, weights, weights, low)


def attend_back(
    own, pieces, x, weights, out_weights, low, q, k, v, ot, logs_in, team, rows, pairs, experts
):
    length, width = x.shape
    local = length // (team * rows)
    share = pairs * PAIR
    block = math.gcd(length, 512)
    unroll = length // block <= 4
    weight, columns, across, logs = attention_specs(length, width, pairs, pairs * team)
    shape = jax.ShapeDtypeStruct
    out = pl.BlockSpec((rows, local, width), lambda p, own: (0, 0, 0))
    results = pl.pallas_call(
        functools.partial(attend_back_kernel, team, rows, local, block, unroll, experts),
        grid_spec=pltpu.PrefetchScalarGridSpec(
            num_scalar_prefetch=1,
            grid=(pairs,),
            in_specs=[fixed(rows, local, width)] * team
            + [fixed(length, width), weight(0), weight(1), weight(2)]
            + [pl.BlockSpec((PAIR, width), lambda p, own: (own[1] * pairs + p, 0))]
            + [fixed(1, length), columns(), columns(), columns(), across, logs],
            out_specs=[out] * team
            + [pl.BlockSpec((experts, 4, width // experts, PAIR), lambda p, own: (0, 0, 0, p))],
            scratch_shapes=[
                pltpu.VMEM((length, width), LOW),
                pltpu.VMEM((length, PAIR), LOW),
                pltpu.VMEM((PAIR, length), LOW),
                pltpu.VMEM((2, length), FULL),
                pltpu.VMEM((PAIR, length), FULL),
                pltpu.VMEM((length, 3 * PAIR), LOW),
                pltpu.VMEM((length, width), FULL),
            ],
        ),
        out_shape=[shape((rows, local, width), LOW)] * team
        + [shape((experts, 4, width // experts, share), LOW)],
        compiler_params=pltpu.CompilerParams(vmem_limit_bytes=VMEM_LIMIT),
        cost_estimate=pl.CostEstimate(
            flops=4 * length * width * 4 * share + 20 * length * length * share,
            bytes_accessed=6 * length * width + 24 * length * share,
            transcendentals=length * length * pairs,
        ),
        name="attend_back",
    )(own, *pieces, x, weights, weights, weights, out_weights, low, q, k, v, ot, logs_in)
    return results[team], results[:team]


GELU_SCALE = math.sqrt(2.0 / math.pi)
GELU_CUBE = 0.044715


def expert_kernel(count, first, last, own_ref, *refs):
    x_refs, refs = refs[:count], refs[count:]
    g_refs, refs = refs[:count], refs[count:]
    up_ref, down_ref, refs = refs[0], refs[1], refs[2:]
    if not first:
        y_in, gx_in, refs = refs[0], refs[1], refs[2:]
    gup_ref, gdown_ref, refs = refs[0], refs[1], refs[2:]
    if last:
        y_out, gx_out, y_sum, gx_sum, refs = refs[0], refs[1], refs[2], refs[3], refs[4:]
    else:
        y_sum, gx_sum, refs = refs[0], refs[1], refs[2:]
    x_ref, g_ref = refs
    step = pl.program_id(0)
    size = x_refs[0].shape[0]

    @pl.when(step == 0)
    def _():
        for index in range(count):
            span = pl.ds(index * size, size)
            x_ref[span, :] = x_refs[index][...]
            g_ref[span, :] = g_refs[index][...]
        if first:
            y_sum[...] = jnp.zeros_like(y_sum)
            gx_sum[...] = jnp.zeros_like(gx_sum)
        else:
            y_sum[...] = y_in[...]
            gx_sum[...] = gx_in[...]

    x = x_ref[...]
    g = g_ref[...]
    inner = dot(x, up_ref[...])
    square = inner * inner
    curve = jnp.tanh(GELU_SCALE * inner * (1.0 + GELU_CUBE * square))
    half = 0.5 + 0.5 * curve
    active = (inner * half).astype(LOW)
    slope = half + (0.5 * GELU_SCALE) * inner * (1.0 - curve * curve) * (
        1.0 + (3.0 * GELU_CUBE) * square
    )
    grad_inner = (dot(g, down_ref[...], NT) * slope).astype(LOW)
    gdown_ref[...] = dot(active, g, TN).astype(LOW)
    gup_ref[...] = dot(x, grad_inner, TN).astype(LOW)
    y_sum[...] += dot(active, down_ref[...])
    gx_sum[...] += dot(grad_inner, up_ref[...], NT)

    if last:

        @pl.when(step == pl.num_programs(0) - 1)
        def _():
            for index in range(count):
                span = pl.ds(index * size, size)
                y_out[own_ref[2] ^ index] = y_sum[span, :].astype(LOW)
                gx_out[own_ref[2] ^ index] = gx_sum[span, :].astype(LOW)


def expert(own, xs, gs, up, down, part, parts, sums):
    count = len(xs)
    size, width = xs[0].shape
    hidden = up.shape[1] // parts
    block = math.gcd(hidden, 512)
    steps = hidden // block
    first, last = part == 0, part == parts - 1
    rows = pl.BlockSpec((size, width), lambda f, own: (0, 0))
    whole = pl.BlockSpec((count * size, width), lambda f, own: (0, 0))
    every = pl.BlockSpec((count, size, width), lambda f, own: (0, 0, 0))
    shape = jax.ShapeDtypeStruct
    sum_shape = shape((count * size, width), FULL)
    in_specs = [rows] * (2 * count) + [
        pl.BlockSpec((width, block), lambda f, own: (0, f + part * steps)),
        pl.BlockSpec((block, width), lambda f, own: (f + part * steps, 0)),
    ]
    out_specs = [
        pl.BlockSpec((width, block), lambda f, own: (0, f)),
        pl.BlockSpec((block, width), lambda f, own: (f, 0)),
    ]
    out_shape = [shape((width, hidden), LOW), shape((hidden, width), LOW)]
    scratch = []
    if not first:
        in_specs += [whole] * 2
    if last:
        out_specs += [every] * 2
        out_shape += [shape((count, size, width), LOW)] * 2
        scratch += [pltpu.VMEM(sum_shape.shape, FULL)] * 2
    else:
        out_specs += [whole] * 2
        out_shape += [sum_shape] * 2
    results = pl.pallas_call(
        functools.partial(expert_kernel, count, first, last),
        grid_spec=pltpu.PrefetchScalarGridSpec(
            num_scalar_prefetch=1,
            grid=(steps,),
            in_specs=in_specs,
            out_specs=out_specs,
            scratch_shapes=scratch + [pltpu.VMEM((count * size, width), LOW)] * 2,
        ),
        out_shape=out_shape,
        compiler_params=pltpu.CompilerParams(vmem_limit_bytes=VMEM_LIMIT),
        cost_estimate=pl.CostEstimate(
            flops=12 * count * size * width * hidden,
            bytes_accessed=8 * width * hidden + 8 * count * size * width,
            transcendentals=count * size * hidden,
        ),
        name="expert",
    )(own, *xs, *gs, up, down, *sums)
    return results[0], results[1], results[2:]


def tie(values, others):
    count, total = len(values), len(values) + len(others)
    return pl.pallas_call(
        lambda *refs: None,
        in_specs=[pl.BlockSpec(memory_space=pl.ANY)] * total,
        out_specs=[pl.BlockSpec(memory_space=pl.ANY)] * count,
        out_shape=[jax.ShapeDtypeStruct(value.shape, value.dtype) for value in values],
        input_output_aliases={index: index for index in range(count)},
        name="tie",
    )(*values, *others)


def put_kernel(count, joined, place, own_ref, *refs):
    out_ref = refs[count + joined]
    size, cut, _ = refs[0].shape
    for i in range(count):
        for n in range(size):
            first = pl.multiple_of(place(own_ref, i, n) * cut, cut)
            out_ref[pl.ds(first, cut), :] = refs[i][n].astype(FULL)


def put_chunk(own, parts, into, shape, block, place):
    count, (size, cut, width) = len(parts), parts[0].shape
    joined = [] if into is None else [into]
    return pl.pallas_call(
        functools.partial(put_kernel, count, len(joined), place),
        grid_spec=pltpu.PrefetchScalarGridSpec(
            num_scalar_prefetch=1,
            grid=(1,),
            in_specs=[pl.BlockSpec((size, cut, width), lambda s, own: (0, 0, 0))] * count
            + [pl.BlockSpec(memory_space=pl.ANY)] * len(joined),
            out_specs=pl.BlockSpec((count * size * cut, width), lambda s, own: block),
        ),
        out_shape=jax.ShapeDtypeStruct(shape, FULL),
        input_output_aliases={1 + count: 0} if joined else {},
        compiler_params=pltpu.CompilerParams(vmem_limit_bytes=VMEM_LIMIT),
        cost_estimate=pl.CostEstimate(
            flops=0, bytes_accessed=8 * count * size * cut * width, transcendentals=0
        ),
        name="put_chunk",
    )(own, *parts, *joined)


def place_kernel(team, rows, experts, own_ref, *refs):
    parts, (qkv_ref, out_ref, hold_ref) = refs[: team * experts], refs[team * experts :]
    cut, share = parts[0].shape[2:]
    which = pl.program_id(0)

    def rows_of(m, k):
        index = (own_ref[2] ^ m) * rows + k
        return pl.ds(pl.multiple_of(index * cut, cut), cut)

    for j in range(team):
        member = lax.rem(own_ref[1] + (team - j), team)
        span = pl.ds(pl.multiple_of(member * share, share), share)

        @pl.when(which < 3)
        def _():
            for m in range(experts):
                for k in range(rows):
                    part = parts[m * team + j][k, 0]
                    qkv_ref[rows_of(m, k), span] = part.astype(FULL)

        @pl.when(which == 3)
        def _():
            for m in range(experts):
                for k in range(rows):
                    part = parts[m * team + j][k, 0]
                    hold_ref[rows_of(m, k), :] = part.astype(FULL)
            out_ref[span, :] = hold_ref[...].T


def place_weights(own, parts, team, rows, experts):
    _, _, cut, share = parts[0].shape
    width, padded = experts * rows * cut, team * share
    return pl.pallas_call(
        functools.partial(place_kernel, team, rows, experts),
        grid_spec=pltpu.PrefetchScalarGridSpec(
            num_scalar_prefetch=1,
            grid=(4,),
            in_specs=[pl.BlockSpec((rows, 1, cut, share), lambda w, own: (0, w, 0, 0))]
            * (team * experts),
            out_specs=[
                pl.BlockSpec((width, padded), lambda w, own: (0, jnp.minimum(w, 2))),
                pl.BlockSpec((padded, width), lambda w, own: (0, 0)),
            ],
            scratch_shapes=[pltpu.VMEM((width, share), FULL)],
        ),
        out_shape=[
            jax.ShapeDtypeStruct((width, 3 * padded), FULL),
            jax.ShapeDtypeStruct((padded, width), FULL),
        ],
        compiler_params=pltpu.CompilerParams(vmem_limit_bytes=VMEM_LIMIT),
        cost_estimate=pl.CostEstimate(
            flops=0, bytes_accessed=24 * width * padded, transcendentals=0
        ),
        name="place_weights",
    )(own, *parts)


def norm_back_kernel(team, own_ref, *refs):
    parts, refs = refs[:team], refs[team:]
    x_ref, more_ref, gain_ref, out_ref, sum_ref = refs
    unit, inverse = standard(x_ref[0].astype(FULL))
    grad = parts[0][0].astype(FULL)
    for part in parts[1:]:
        grad = grad + part[0].astype(FULL)
    back, gain, bias = standard_back(grad, gain_ref[...], unit, inverse)
    out_ref[0] = (back + more_ref[0].astype(FULL)).astype(LOW)

    @pl.when(pl.program_id(0) == 0)
    def _():
        sum_ref[...] = jnp.zeros_like(sum_ref)

    sum_ref[0:1, :] += gain[None]
    sum_ref[1:2, :] += bias[None]


def norm_back(own, parts, x, more, gain):
    rows, local, width = x.shape
    block = pl.BlockSpec((1, local, width), lambda k, own: (k, 0, 0))
    home = lambda k, own: (lax.rem(own[0] + (rows - k), rows), 0, 0)
    return pl.pallas_call(
        functools.partial(norm_back_kernel, len(parts)),
        grid_spec=pltpu.PrefetchScalarGridSpec(
            num_scalar_prefetch=1,
            grid=(rows,),
            in_specs=[block] * (len(parts) + 2)
            + [pl.BlockSpec((1, width), lambda k, own: (0, 0))],
            out_specs=[
                pl.BlockSpec((1, local, width), home),
                pl.BlockSpec((8, width), lambda k, own: (0, 0)),
            ],
        ),
        out_shape=[
            jax.ShapeDtypeStruct(x.shape, LOW),
            jax.ShapeDtypeStruct((8, width), FULL),
        ],
        cost_estimate=pl.CostEstimate(flops=0, bytes_accessed=40 * x.size, transcendentals=0),
        name="norm_back",
    )(own, *parts, x, more, gain[None])


def add_low(a, b):
    return (a.astype(FULL) + b.astype(FULL)).astype(LOW)


def pick(value, index):
    return lax.dynamic_index_in_dim(value, index, 0, keepdims=False)


def ring_scatter(value, size, place, send):
    total = pick(value, (place + size - 1) % size)
    for step in range(size - 1):
        total = add_low(send(total), pick(value, (place + 2 * size - 2 - step) % size))
    return total


def ring_gather(value, size, place, send):
    out = jnp.zeros((size,) + value.shape, value.dtype)
    out = lax.dynamic_update_index_in_dim(out, value, place, 0)
    for step in range(size - 1):
        value = send(value)
        out = lax.dynamic_update_index_in_dim(out, value, (place + size - 1 - step) % size, 0)
    return out


def per_device(
    block_input, segment_ids, expert_ids, ln1_gain, ln1_bias, ln2_gain, ln2_bias,
    w_qkv, w_attn_out, w_in, w_down, grad_out,
):
    rows, local, width = block_input.shape
    seq = lax.axis_size("seq")
    experts = lax.axis_size("ex")
    team = seq // rows
    length = seq * local
    owned = rows * local
    pairs = -(-HEADS // (2 * team))
    share = pairs * PAIR
    padded = share * team
    place = lax.axis_index("seq")
    mine = lax.axis_index("ex")
    row, member = place // team, place % team
    slots = rows * MOST

    def row_send(value, k):
        if k % rows == 0:
            return value
        pattern = [(a * team + b, (a + k) % rows * team + b) for a in range(rows) for b in range(team)]
        return lax.ppermute(value, "seq", pattern)

    def team_send(value, j):
        if j % team == 0:
            return value
        pattern = [(a * team + b, a * team + (b + j) % team) for a in range(rows) for b in range(team)]
        return lax.ppermute(value, "seq", pattern)

    def swap(value, axis, m):
        if m == 0 or m >= lax.axis_size(axis):
            return value
        return lax.ppermute(value, axis, [(a, a ^ m) for a in range(lax.axis_size(axis))])

    across_rows = [[r * team + g for r in range(rows)] for g in range(team)]

    def swap_rows(value):
        return lax.all_to_all(value, "seq", 0, 0, tiled=True, axis_index_groups=across_rows)

    def swap_experts(value):
        return lax.all_to_all(value, "ex", 0, 0, tiled=True)

    center = (block_input - jnp.mean(block_input, -1, keepdims=True)).astype(LOW)
    owned_x = [row_send(pick(center, (row + k) % rows), k) for k in range(rows)]
    pieces = [team_send(piece, j) for j in range(team) for piece in owned_x]

    labels = jnp.pad(expert_ids.reshape(rows, 1, local), ((0, 0), (0, 15), (0, width - local)))
    carried = jnp.concatenate([grad_out.astype(LOW), labels.astype(LOW)], 1)
    carried = tie([carried], [owned_x[1]])[0]
    owned_g = jnp.stack([row_send(pick(carried, (row + k) % rows), k) for k in range(rows)])
    grad_low = owned_g[:, :local]
    chosen = owned_g[:, local, :local].astype(jnp.int32)

    segments = lax.dynamic_slice_in_dim(segment_ids, row, 1, 0)[0]
    lows = jnp.sum((segments[:, None] < segments[None, :]).astype(jnp.int32), 0)[None, :]

    weights, out_weights = w_qkv, w_attn_out
    if padded != width:
        extra = padded - width
        weights = jnp.pad(w_qkv.reshape(width, 3, width), ((0, 0), (0, 0), (0, extra)))
        weights = weights.reshape(width, 3 * padded)
        out_weights = jnp.pad(w_attn_out, ((0, extra), (0, 0)))

    own = jnp.stack([row, member, mine]).astype(jnp.int32)
    results = attend(own, pieces, ln1_gain, ln1_bias, weights, lows, team, rows, pairs)
    full, q, k, v, ot, logs = results[:6]
    branch = 0.0
    for j, part in enumerate(tie(results[6:], [owned_g])):
        first = (member + team - j) % team * share
        weight = lax.dynamic_slice_in_dim(out_weights, first, share, 0)
        branch = branch + dot(team_send(part, j).reshape(owned, share), weight)

    residual = jnp.concatenate(owned_x, 0).astype(FULL)
    middle = residual + branch
    unit_two, inverse_two = standard(middle)
    normed_two = (unit_two * ln2_gain + ln2_bias).astype(LOW)

    relative = chosen ^ mine
    onehot = (relative[..., None] == jnp.arange(experts, dtype=jnp.int32)).astype(jnp.int32)
    rank = jnp.cumsum(onehot, 1) - onehot
    target = relative * MOST + jnp.sum(rank * onehot, -1)
    numbers = jnp.arange(experts * MOST, dtype=jnp.int32)[None, :, None]

    def routes(target):
        match = (target[:, None, :] == numbers).astype(LOW)
        return match.reshape(rows, experts, MOST, local)

    route = routes(target)
    back_route = routes((target // MOST ^ mine) * MOST + target % MOST)
    named = (chosen[..., None] == jnp.arange(experts, dtype=jnp.int32)).astype(FULL)
    counts = jnp.sum(named, (0, 1))

    def dispatch(value):
        placed = jnp.einsum(
            "remt,rtd->ermd", route, value.reshape(rows, local, width), preferred_element_type=FULL
        )
        placed = placed.astype(LOW).reshape(experts, slots, width)
        return [swap(placed[m], "ex", m) for m in range(experts)]

    def collect(returned):
        return jnp.einsum(
            "remt,ermd->rtd",
            back_route,
            returned.reshape(experts, rows, MOST, width),
            preferred_element_type=FULL,
        ).reshape(owned, width)

    grad_arrived = dispatch(grad_low)
    arrived = dispatch(normed_two)

    hops = rows - 1

    def along_team(value):
        return team_send(value, 1)

    def team_scatter(value):
        return ring_scatter(value, team, member, along_team)

    def team_gather(value):
        return [team_send(value, j) for j in range(team)]

    def cut_up(value, sizes):
        return value.reshape(sizes + (value.shape[0] // seq,) + value.shape[1:])

    def first_hop(value):
        return row_send(pick(value, (row + rows - 1) % rows), 1)

    def joined(came, value, step):
        return add_low(came, pick(value, (row + 2 * rows - 2 - step) % rows))

    def next_hop(came, value, step):
        return row_send(joined(came, value, step), 1)

    def sync(*values):
        leaves, tree = jax.tree.flatten(values)
        return jax.tree.unflatten(tree, tie(leaves, []))

    def team_first(own_ref, i, n):
        device = lax.rem(own_ref[1] + (team - i), team)
        return device * rows + lax.rem(own_ref[0] + (rows - n), rows)

    def rows_first(own_ref, i, n):
        device = lax.rem(own_ref[1] + (team - n), team)
        return lax.rem(own_ref[0] + (rows - i), rows) * team + device

    up_shape, down_shape = w_in.shape[1:], w_down.shape[1:]

    up_one, down_one, sums = expert(own, arrived, grad_arrived, w_in[0], w_down[0], 0, 2, ())
    cut_a = cut_up(up_one, (team, rows))
    cut_z = cut_up(down_one, (rows, team))
    half_a = team_scatter(cut_a)
    z = first_hop(cut_z)
    up_two, down_two, sums = expert(own, arrived, grad_arrived, w_in[0], w_down[0], 1, 2, sums)
    produced, grad_rows = sums
    z, produced, grad_rows = sync(z, produced, grad_rows)

    grad_rows = swap_experts(grad_rows)
    z = next_hop(z, cut_z, 0)
    grad_rows, produced, half_a = sync(grad_rows, produced, half_a)

    produced = swap_experts(produced)
    back_two, grad_gain_two, grad_bias_two = standard_back(
        collect(grad_rows), ln2_gain, unit_two, inverse_two
    )
    grad_branch = (back_two + grad_low.reshape(owned, width).astype(FULL)).astype(LOW)
    grad_branch = grad_branch.reshape(rows, local, width)
    grad_branch, z = sync(grad_branch, z)

    branches = [team_send(grad_branch, j) for j in range(team)]
    z = next_hop(z, cut_z, 1)
    half_a, up_two, down_two = sync(half_a, up_two, down_two)

    a = first_hop(half_a)
    half_b = team_scatter(cut_up(up_two, (team, rows)))
    z, produced = sync(z, produced)

    z = joined(z, cut_z, 2)
    change = (branch + collect(produced)).astype(LOW).reshape(rows, local, width)
    change = jnp.stack([change[(rows - n) % rows] for n in range(rows)] * 2)
    change = lax.dynamic_slice_in_dim(change, (rows - row) % rows, rows, 0)
    a, change = sync(a, change)

    a = next_hop(a, half_a, 0)
    branches, down_two, change = sync(branches, down_two, change)

    change = swap_rows(change)
    half_c = team_scatter(cut_up(down_two, (team, rows)))
    grads, grad_full = attend_back(
        own, branches, full, weights, out_weights, lows, q, k, v, ot, logs,
        team, rows, pairs, experts,
    )
    half_b, a, z, grads, grad_full = sync(half_b, a, z, grads, grad_full)

    grads = swap_experts(grads)
    grad_full = [team_send(part, j) for j, part in enumerate(grad_full)]
    b = first_hop(half_b)
    a = next_hop(a, half_a, 1)
    change, half_c, a, z = sync(change, half_c, a, z)

    a = joined(a, half_a, 2)
    pieces_a = [a, row_send(a, 1)]
    z = team_scatter(z)
    block_output = block_input + change.astype(FULL)
    b, block_output = sync(b, block_output)

    b = next_hop(b, half_b, 0)
    pieces_a = sync(pieces_a)[0]

    pieces_a = pieces_a + [row_send(pieces_a[-1], 1)]
    b, grads = sync(b, grads)

    b = next_hop(b, half_b, 1)
    cut = width // (experts * rows)
    grads = jnp.sum(grads.astype(FULL), 0).astype(LOW).reshape(4, rows, cut, share)
    grads = swap_rows(grads.swapaxes(0, 1))
    pieces_a, grad_full = sync(pieces_a, grad_full)

    pieces_a = pieces_a + [row_send(pieces_a[-1], 1)]
    grad_change, norm_sums = norm_back(
        own, grad_full, jnp.stack(owned_x), back_two.reshape(rows, local, width), ln1_gain
    )
    b, z, grad_change, norm_sums = sync(b, z, grad_change, norm_sums)

    b = joined(b, half_b, 2)
    pieces_b = [b, row_send(b, 1)]
    z = jnp.stack(team_gather(z))
    small = jnp.stack(
        [
            norm_sums[0], norm_sums[1], grad_gain_two, grad_bias_two,
            jnp.pad(counts, (0, width - experts)),
        ]
    )
    small = small + swap(small, "ex", 1)
    pieces_a, half_c = sync(pieces_a, half_c)

    c = first_hop(half_c)
    all_a = team_gather(jnp.stack(pieces_a))
    pieces_b, grads = sync(pieces_b, grads)

    pieces_b = pieces_b + [row_send(pieces_b[-1], 1)]
    grads = jnp.sum(grads.astype(FULL), 0).astype(LOW)
    grads = swap_rows(jnp.broadcast_to(grads[None], (rows,) + grads.shape))
    c, small = sync(c, small)

    c = next_hop(c, half_c, 0)
    small = small + swap(small, "ex", 2)
    pieces_b = sync(pieces_b)[0]

    pieces_b = pieces_b + [row_send(pieces_b[-1], 1)]
    c, z = sync(c, z)

    c = next_hop(c, half_c, 1)
    pieces_b, grads, all_a = sync(pieces_b, grads, all_a)

    share_grads = team_gather(grads)
    all_b = team_gather(jnp.stack(pieces_b))
    pieces_z = [z, row_send(z, 1)]
    grad_up = put_chunk(own, all_a, None, up_shape, (0, 0), team_first)
    c, small, grad_up = sync(c, small, grad_up)

    c = joined(c, half_c, 2)
    pieces_c = [c, row_send(c, 1)]
    for bit in range(team.bit_length() - 1):
        small = small + swap(small, "seq", 1 << bit)
    pieces_z = sync(pieces_z)[0]

    pieces_z = pieces_z + [row_send(pieces_z[-1], 1)]
    pieces_c, share_grads = sync(pieces_c, share_grads)

    pieces_c = pieces_c + [row_send(pieces_c[-1], 1)]
    far_grads = [swap(part, "ex", 2) for part in share_grads]
    pieces_z, small, grad_change = sync(pieces_z, small, grad_change)

    pieces_z = pieces_z + [row_send(pieces_z[-1], 1)]
    pieces_c, all_b, far_grads, share_grads = sync(pieces_c, all_b, far_grads, share_grads)

    pieces_c = pieces_c + [row_send(pieces_c[-1], 1)]
    near = [swap(part, "ex", 1) for part in share_grads]
    far = [swap(part, "ex", 1) for part in far_grads]
    grad_up = put_chunk(own, all_b, grad_up, up_shape, (0, 1), team_first)
    pieces_z, grad_up = sync(pieces_z, grad_up)

    grad_change = swap_rows(grad_change)
    parts = share_grads + near + far_grads + far
    grad_qkv, grad_attn_out = place_weights(own, parts, team, rows, experts)
    pieces_c, grad_qkv = sync(pieces_c, grad_qkv)

    all_c = team_gather(jnp.stack(pieces_c))
    grad_down = put_chunk(own, pieces_z, None, down_shape, (0, 0), rows_first)
    grad_input = grad_out + grad_change.astype(FULL)
    all_c, grad_qkv, grad_input, grad_down, small = sync(
        all_c, grad_qkv, grad_input, grad_down, small
    )
    small = sum(row_send(small, k) for k in range(rows))

    if padded != width:
        grad_qkv = grad_qkv.reshape(width, 3, padded)[..., :width].reshape(width, 3 * width)
        grad_attn_out = grad_attn_out[:width]
    grad_down = put_chunk(own, all_c, grad_down, down_shape, (1, 0), team_first)
    load = small[4, :experts] * (experts / (rows * length * experts))
    return (
        block_output, grad_input, grad_qkv, grad_attn_out, small[0], small[1], small[2],
        small[3], grad_up[None], grad_down[None], load,
    )


def solution(mesh):
    tokens = P("ex", "seq", None)
    expert_axis = P("ex", None, None)
    return jax.shard_map(
        per_device,
        mesh=mesh,
        in_specs=(
            tokens, P("ex", None), tokens, P(), P(), P(), P(), P(), P(),
            expert_axis, expert_axis, tokens,
        ),
        out_specs=(
            tokens, tokens, P(), P(), P(), P(), P(), P(), expert_axis, expert_axis, P(),
        ),
        check_vma=False,
    )
```
